256 devices in a mesh: gx: 4 (over y), gy: 4 (over z_lo, core), gz: 16 (over z_hi, x).
Axes of the slice: x: 4, y: 4, z: 8 (z_hi: 4, z_lo: 2; z = z_hi * 2 + z_lo), core: 2. Of those that a mesh axis runs over, the one named last changes fastest.
Arguments:
- positions: float32 [4, 16, 16, 3, 128], P('gx', 'gy', 'gz'), may hold values from 0 to 1
- velocities: float32 [4, 16, 16, 3, 128], P('gx', 'gy', 'gz'), may hold values from -6 to 6
- charges: float32 [4, 16, 16, 128], P('gx', 'gy', 'gz'), may hold values from -3 to 3
- atom_types: int32 [4, 16, 16, 128], P('gx', 'gy', 'gz'), may hold values from 0 to 15
- atom_count: int32 [4, 16, 16], P('gx', 'gy', 'gz'), may hold values from 32 to 128
- sigma_type: float32 [16], replicated, may hold values from 0.15 to 0.35
- epsilon_type: float32 [16], replicated, may hold values from 0.3 to 3
- masses: float32 [4, 16, 16, 128], P('gx', 'gy', 'gz'), may hold values from 1 to 4
- pair_list: int32 [4, 4, 16, 2, 56], P('gx', 'gy', 'gz'), may hold values from 0 to 19, as said below
- pair_count: int32 [4, 4, 16], P('gx', 'gy', 'gz'), may hold values from 1 to 56, as said below
- pos_cotangent: float32 [4, 16, 16, 3, 128], P('gx', 'gy', 'gz'), may hold values from -6 to 6
- vel_cotangent: float32 [4, 16, 16, 3, 128], P('gx', 'gy', 'gz'), may hold values from -6 to 6
Outputs:
- pos_final: float32 [4, 16, 16, 3, 128], P('gx', 'gy', 'gz')
- vel_final: float32 [4, 16, 16, 3, 128], P('gx', 'gy', 'gz')
- grad_pos: float32 [4, 16, 16, 3, 128], P('gx', 'gy', 'gz')
- grad_vel: float32 [4, 16, 16, 3, 128], P('gx', 'gy', 'gz')
- grad_charge: float32 [4, 16, 16, 128], P('gx', 'gy', 'gz')
The draws below stay inside these ranges and needn't reach their ends.
Inputs may be any that keep to these rules, and one draw needn't show every extreme that they name: `pair_list`: for k < pair_count[a, b, c] the two extended indices of slot k name blocks inside the global grid of 4 x 16 x 16 blocks, their coordinates differ by at most one in each dimension, and their smaller coordinate in each dimension lies in the device's own blocks; an unordered pair of blocks appears in at most one live slot over all devices. Slots at and past the count hold indices in range and are ignored. `pair_count`: some device has all 56 slots live in every draw.
All inputs are finite; a program needn't handle non-finite values.
Results may differ from the reference program's by a relative error of at most 0.00027.
Values sent between devices are 32-bit elements; how exact they have to be, the bound alone decides.
No kernel may reach another device: no remote copies, remote signals or barrier semaphores. Data moves between devices by JAX's collectives and lax.ppermute only.
A program may use at most 64 MiB of HBM per device.

```python
import math
import jax
import jax.numpy as jnp
import numpy as np
from jax import lax

BX = 1
BY = 4
BZ = 1
ATOMS = 128
NTYPES = 16
STEPS = 5
NX = 4
NY = 16
NZ = 16


def corner_pairs():
    options = ((0, 0), (0, 1), (1, 0))
    lefts = []
    rights = []
    for option_x in options:
        for option_y in options:
            for option_z in options:
                left_corner = (option_x[0], option_y[0], option_z[0])
                right_corner = (option_x[1], option_y[1], option_z[1])
                if left_corner <= right_corner:
                    lefts.append(left_corner)
                    rights.append(right_corner)
    return (np.array(lefts, dtype=np.int32), np.array(rights, dtype=np.int32))


def pair_tables(key):
    grid_x = NX // BX
    grid_y = NY // BY
    grid_z = NZ // BZ
    lefts, rights = corner_pairs()
    own_cells = np.array([[cell_x, cell_y, cell_z] for cell_x in range(BX) for cell_y in range(BY) for cell_z in range(BZ)], dtype=np.int32)
    cand_left = (own_cells[:, None, :] + lefts[None, :, :]).reshape(-1, 3)
    cand_right = (own_cells[:, None, :] + rights[None, :, :]).reshape(-1, 3)
    slot_total = cand_left.shape[0]

    def ext_index(coords):
        return ((coords[:, 0] * (BY + 1) + coords[:, 1]) * (BZ + 1) + coords[:, 2]).astype(np.int32)
    anchors = np.array([[dev_x * BX, dev_y * BY, dev_z * BZ] for dev_x in range(grid_x) for dev_y in range(grid_y) for dev_z in range(grid_z)], dtype=np.int32)
    highest = jnp.maximum(jnp.asarray(cand_left), jnp.asarray(cand_right))
    limits = jnp.asarray(np.array([NX, NY, NZ], dtype=np.int32))
    inside = jnp.all(jnp.asarray(anchors)[:, None, :] + highest[None, :, :] < limits, axis=-1)
    inside_total = jnp.sum(inside.astype(jnp.int32), axis=1).astype(jnp.int32)
    device_total = anchors.shape[0]
    shuffled = jax.vmap(lambda sub_key: jax.random.permutation(sub_key, slot_total))(jax.random.split(jax.random.fold_in(key, 11), device_total))
    scores = (jnp.where(inside, 0, slot_total) + shuffled).astype(jnp.int32)
    ordering = jnp.argsort(scores, axis=1, stable=True)
    left_ids = jnp.asarray(ext_index(cand_left))[ordering]
    right_ids = jnp.asarray(ext_index(cand_right))[ordering]
    reversal = jax.random.randint(jax.random.fold_in(key, 12), (device_total, slot_total), 0, 2)
    firsts = jnp.where(reversal == 1, right_ids, left_ids)
    seconds = jnp.where(reversal == 1, left_ids, right_ids)
    levels = jax.random.randint(jax.random.fold_in(key, 13), (device_total,), 1, 9)
    counts = jnp.maximum(slot_total * levels * levels // 64, 1)
    counts = jnp.minimum(counts, inside_total)
    counts = counts.at[device_total - 1].set(1)
    counts = counts.at[0].set(inside_total[0])
    return (firsts, seconds, counts, (grid_x, grid_y, grid_z, slot_total))


def draw_pair_list(key, part):
    firsts, seconds, counts, extents = pair_tables(key)
    stacked = jnp.stack([firsts, seconds], axis=1)
    return stacked.reshape(extents[0], extents[1], extents[2], 2, extents[3]).astype(jnp.int32)


def draw_pair_count(key, part):
    firsts, seconds, counts, extents = pair_tables(key)
    return counts.reshape(extents[0], extents[1], extents[2]).astype(jnp.int32)


def with_ends(values, own_key, smallest, high):
    spot = [jax.random.randint(jax.random.fold_in(own_key, axis), (), 0, length) for axis, length in enumerate(values.shape)]
    main_axis = values.shape.index(max(values.shape))
    next_to = spot[:main_axis] + [(spot[main_axis] + 1) % values.shape[main_axis]] + spot[main_axis + 1:]
    return values.at[tuple(spot)].set(smallest).at[tuple(next_to)].set(high)


def block_scale(rng, shape, pieces, least, high):
    def one(dim, blocks):
        heights = jax.random.uniform(jax.random.fold_in(jax.random.fold_in(rng, 6), dim), (blocks,), jnp.float32, least / len(pieces), high / len(pieces))
        return jnp.repeat(jnp.exp(heights), shape[dim] // blocks).reshape((-1,) + (1,) * (len(shape) - dim - 1))

    gain = one(*pieces[0])
    for cut in pieces[1:]:
        gain = gain * one(*cut)
    return gain


def noise(rng, shape, deviation, reach, pieces=(), kind=jnp.bfloat16):
    result = deviation * jax.random.normal(rng, shape, jnp.float32)
    if pieces:
        result = result * block_scale(rng, shape, pieces, -0.22, 0.18)
    return jnp.clip(result, -reach, reach).astype(kind)


def setup_inputs(seed: int = 0) -> dict:
    key_list = jax.random.split(jax.random.key(seed), 13)
    return {
        "positions": jnp.clip(1.0 * jax.random.uniform(key_list[0], (NX, NY, NZ, 3, ATOMS), jnp.float32) ** block_scale(key_list[0], (NX, NY, NZ, 3, ATOMS), ((0, 4), (1, 4), (2, 16)), -0.2, 0.2), 0.0, 1.0),
        "velocities": noise(key_list[1], (NX, NY, NZ, 3, ATOMS), 1.0, 6.0, ((0, 4), (1, 4), (2, 16)), jnp.float32),
        "charges": noise(key_list[2], (NX, NY, NZ, ATOMS), 0.5, 3.0, ((0, 4), (1, 4), (2, 16)), jnp.float32),
        "atom_types": with_ends(jax.random.randint(key_list[3], (NX, NY, NZ, ATOMS), 0, NTYPES), jax.random.fold_in(key_list[3], 1), 0, NTYPES - 1).astype(jnp.int32),
        "atom_count": with_ends(jax.random.randint(key_list[4], (NX, NY, NZ), ATOMS // 4, ATOMS + 1), jax.random.fold_in(key_list[4], 1), ATOMS // 4, ATOMS).astype(jnp.int32),
        "sigma_type": jnp.clip(jnp.exp(jax.random.uniform(key_list[5], (NTYPES,), jnp.float32, math.log(0.15), math.log(0.35))), 0.15, 0.35),
        "epsilon_type": jnp.clip(jnp.exp(jax.random.uniform(key_list[6], (NTYPES,), jnp.float32, math.log(0.3), math.log(3.0))), 0.3, 3.0),
        "masses": jnp.clip(jnp.exp(math.log(4.0) - 1.3862944 * jax.random.uniform(key_list[7], (NX, NY, NZ, ATOMS), jnp.float32) ** block_scale(key_list[7], (NX, NY, NZ, ATOMS), ((0, 4), (1, 4), (2, 16)), -0.2, 0.2)), 1.0, 4.0),
        "pair_list": draw_pair_list(jax.random.fold_in(key_list[12], 71), 0),
        "pair_count": draw_pair_count(jax.random.fold_in(key_list[12], 71), 0),
        "pos_cotangent": noise(key_list[10], (NX, NY, NZ, 3, ATOMS), 1.0, 6.0, ((0, 4), (1, 4), (2, 16)), jnp.float32),
        "vel_cotangent": noise(key_list[11], (NX, NY, NZ, 3, ATOMS), 1.0, 6.0, ((0, 4), (1, 4), (2, 16)), jnp.float32),
    }


SOFT = 0.04
KAPPA = 2.0
COULOMB = 4.0
TIME_STEP = 0.004

def tile_energy(left_pos, right_pos, left_charge, right_charge, left_sigma, right_sigma, left_depth, right_depth, offset, same_block):
    separation = left_pos[:, :, None] - right_pos[:, None, :] + offset[:, None, None]
    distance = lax.optimization_barrier(jnp.sum(separation * separation, axis=0))
    mean_sigma = 0.5 * (left_sigma[:, None] + right_sigma[None, :])
    squared_sigma = mean_sigma * mean_sigma
    fraction = squared_sigma / (distance + squared_sigma)
    third_power = fraction * fraction * fraction
    dispersion = 4.0 * left_depth[:, None] * right_depth[None, :] * (third_power * third_power - third_power)
    radius = jnp.sqrt(distance + SOFT)
    screened = COULOMB * left_charge[:, None] * right_charge[None, :] * jnp.exp(-KAPPA * radius) / radius
    fading = jnp.maximum(1.0 - distance, 0.0)
    switch = fading * fading * fading
    per_block = left_pos.shape[1]
    diagonal = (lax.broadcasted_iota(jnp.int32, (per_block, per_block), 0) == lax.broadcasted_iota(jnp.int32, (per_block, per_block), 1)).astype(jnp.float32)
    weight = 1.0 - same_block * (0.5 + 0.5 * diagonal)
    return jnp.sum(weight * switch * (dispersion + screened))

def tile_forces(left_pos, right_pos, left_charge, right_charge, left_sigma, right_sigma, left_depth, right_depth, offset, same_block):
    gradients = jax.grad(tile_energy, argnums=(0, 1))(left_pos, right_pos, left_charge, right_charge, left_sigma, right_sigma, left_depth, right_depth, offset, same_block)
    return (-gradients[0], -gradients[1])

def pair_terms(flat_pos, flat_par, flat_cot, first_ids, second_ids, offset, same_block, live_slot, with_forces):
    left_pos = jnp.take(flat_pos, first_ids, axis=0)
    right_pos = jnp.take(flat_pos, second_ids, axis=0)
    left_par = jnp.take(flat_par, first_ids, axis=0)
    right_par = jnp.take(flat_par, second_ids, axis=0)
    slot_mask = live_slot[:, None, None]

    def batch_forces(pos_one, pos_two, charge_one, charge_two):
        return jax.vmap(tile_forces)(pos_one, pos_two, charge_one, charge_two, left_par[:, 1], right_par[:, 1], left_par[:, 2], right_par[:, 2], offset, same_block)
    if flat_cot is None:
        left_force, right_force = batch_forces(left_pos, right_pos, left_par[:, 0], right_par[:, 0])
        return (left_force * slot_mask, right_force * slot_mask)
    results, pullback = jax.vjp(batch_forces, left_pos, right_pos, left_par[:, 0], right_par[:, 0])
    left_cot = jnp.take(flat_cot, first_ids, axis=0) * slot_mask
    right_cot = jnp.take(flat_cot, second_ids, axis=0) * slot_mask
    pulled = pullback((left_cot, right_cot))
    left_rows = [pulled[0], pulled[2][:, None, :]]
    right_rows = [pulled[1], pulled[3][:, None, :]]
    if with_forces:
        left_rows = [results[0] * slot_mask] + left_rows
        right_rows = [results[1] * slot_mask] + right_rows
    return (jnp.concatenate(left_rows, axis=1), jnp.concatenate(right_rows, axis=1))

def atom_params(charges, atom_types, atom_count, sigma_type, epsilon_type):
    type_total = sigma_type.shape[0]
    alive_mask = (lax.broadcasted_iota(jnp.int32, charges.shape, charges.ndim - 1) < atom_count[..., None]).astype(jnp.float32)
    matches = (atom_types[..., None, :] == lax.broadcasted_iota(jnp.int32, (type_total, 1), 0)).astype(jnp.float32)
    sigma_atom = lax.optimization_barrier(jnp.sum(matches * sigma_type[:, None], axis=-2))
    depth_atom = lax.optimization_barrier(jnp.sum(matches * epsilon_type[:, None], axis=-2))
    params = jnp.stack([charges * alive_mask, sigma_atom, jnp.sqrt(depth_atom) * alive_mask], axis=-2)
    return (alive_mask, params)

def global_pairs(pair_list, pair_count):
    grid_x, grid_y, grid_z, unused, slot_total = pair_list.shape
    grid_shape = (grid_x, grid_y, grid_z, slot_total)

    def local_coords(index):
        return (index // ((BY + 1) * (BZ + 1)), index // (BZ + 1) % (BY + 1), index % (BZ + 1))
    anchor_x = lax.broadcasted_iota(jnp.int32, grid_shape, 0) * BX
    anchor_y = lax.broadcasted_iota(jnp.int32, grid_shape, 1) * BY
    anchor_z = lax.broadcasted_iota(jnp.int32, grid_shape, 2) * BZ
    left_local = local_coords(pair_list[:, :, :, 0, :])
    right_local = local_coords(pair_list[:, :, :, 1, :])

    def global_index(coords):
        return ((coords[0] + anchor_x) * NY + (coords[1] + anchor_y)) * NZ + (coords[2] + anchor_z)
    live_grid = lax.broadcasted_iota(jnp.int32, grid_shape, 3) < pair_count[..., None]
    zero_ids = jnp.zeros(grid_shape, jnp.int32)
    first_ids = jnp.where(live_grid, global_index(left_local).astype(jnp.int32), zero_ids).astype(jnp.int32).reshape(-1)
    second_ids = jnp.where(live_grid, global_index(right_local).astype(jnp.int32), zero_ids).astype(jnp.int32).reshape(-1)
    offsets = jnp.stack([(left_local[column] - right_local[column]).astype(jnp.float32) for column in range(3)], axis=-1).reshape(-1, 3)
    same_block = (pair_list[:, :, :, 0, :] == pair_list[:, :, :, 1, :]).astype(jnp.float32).reshape(-1)
    live_slot = live_grid.astype(jnp.float32).reshape(-1)
    return (first_ids, second_ids, offsets, same_block, live_slot)

def reference(positions, velocities, charges, atom_types, atom_count, sigma_type, epsilon_type, masses, pair_list, pair_count, pos_cotangent, vel_cotangent):
    alive_mask, params = atom_params(charges, atom_types, atom_count, sigma_type, epsilon_type)
    blocks_total = NX * NY * NZ
    per_block = positions.shape[-1]
    flat_par = params.reshape(blocks_total, 3, per_block)
    first_ids, second_ids, offsets, same_block, live_slot = global_pairs(pair_list, pair_count)
    group = pair_list.shape[-1]
    batches = (first_ids.reshape(-1, group), second_ids.reshape(-1, group), offsets.reshape(-1, group, 3), same_block.reshape(-1, group), live_slot.reshape(-1, group))

    def evaluate(flat_pos, flat_cot):
        rows_total = 3 if flat_cot is None else 4

        def one_batch(totals, batch):
            first_batch, second_batch, offset_batch, same_batch, slot_batch = batch
            left_rows, right_rows = pair_terms(flat_pos, flat_par, flat_cot, first_batch, second_batch, offset_batch, same_batch, slot_batch, False)
            totals = totals.at[first_batch].add(left_rows).at[second_batch].add(right_rows)
            return (totals, None)
        totals, unused = lax.scan(one_batch, jnp.zeros((blocks_total, rows_total, per_block), jnp.float32), batches)
        return totals
    inverse = (1.0 / masses).reshape(blocks_total, 1, per_block)
    half_step = 0.5 * TIME_STEP
    position = positions.reshape(blocks_total, 3, per_block)
    velocity = velocities.reshape(blocks_total, 3, per_block)
    history = [position]
    forces = evaluate(position, None)
    for step_index in range(STEPS):
        midway = velocity + half_step * inverse * forces
        position = position + TIME_STEP * midway
        history.append(position)
        forces = evaluate(position, None)
        velocity = midway + half_step * inverse * forces
    grad_position = pos_cotangent.reshape(blocks_total, 3, per_block)
    grad_velocity = vel_cotangent.reshape(blocks_total, 3, per_block)
    charge_sum = jnp.zeros((blocks_total, per_block), jnp.float32)
    pulled = evaluate(history[STEPS], half_step * inverse * grad_velocity)
    grad_position = grad_position + pulled[:, :3]
    charge_sum = charge_sum + pulled[:, 3]
    for step_index in range(STEPS - 1, -1, -1):
        grad_velocity = grad_velocity + TIME_STEP * grad_position
        factor = TIME_STEP if step_index > 0 else half_step
        pulled = evaluate(history[step_index], factor * inverse * grad_velocity)
        grad_position = grad_position + pulled[:, :3]
        charge_sum = charge_sum + pulled[:, 3]
    grad_charge = charge_sum * alive_mask.reshape(blocks_total, per_block)
    vector_shape = (NX, NY, NZ, 3, per_block)
    return (position.reshape(vector_shape), velocity.reshape(vector_shape), grad_position.reshape(vector_shape), grad_velocity.reshape(vector_shape), grad_charge.reshape(NX, NY, NZ, per_block))
```

```python
import functools

import jax
import jax.numpy as jnp
from jax import lax
from jax.experimental import pallas as pl
from jax.experimental.pallas import tpu as pltpu
from jax.sharding import PartitionSpec as P

STEPS = 5
SOFT = 0.04
KAPPA = 2.0
COULOMB = 4.0
TIME_STEP = 0.004
HALF = 0.5 * TIME_STEP
AXES = ("gx", "gy", "gz")
GRID = 16
BLOCKS = 16
ROWS = 18
TILES = 4
GROUP = 8 * TILES


def column_device(y, z):
    phys_y = y // 4
    phys_x = y % 4 if phys_y % 2 == 0 else 3 - y % 4
    phys_z = z // 2
    core = z % 2 if phys_z % 2 == 0 else 1 - z % 2
    return (phys_y * 4 + (phys_z % 2) * 2 + core) * 16 + (phys_z // 2) * 4 + phys_x


def column_of_device():
    gx, gy, gz = (lax.axis_index(name) for name in AXES)
    low, core = gy // 2, gy % 2
    high, phys_x = gz // 4, gz % 4
    phys_z = high * 2 + low
    y = gx * 4 + jnp.where(gx % 2 == 0, phys_x, 3 - phys_x)
    z = phys_z * 2 + jnp.where(phys_z % 2 == 0, core, 1 - core)
    return y, z


def spread_pairs(turn):
    return [
        ((a * 4 + b) * 16 + c, column_device(4 * b + (a + turn) % 4, c))
        for a in range(4)
        for b in range(4)
        for c in range(16)
    ]


def swap_pairs(axis, parity):
    pairs = []
    for y in range(GRID):
        for z in range(GRID):
            own = (y, z)[axis]
            other = own + 1 if own % 2 == parity else own - 1
            if 0 <= other < GRID:
                target = (other, z) if axis == 0 else (y, other)
                pairs.append((column_device(y, z), column_device(*target)))
    return pairs


def down_pairs(axis):
    pairs = []
    for y in range(GRID):
        for z in range(GRID):
            target = (y - 1, z) if axis == 0 else (y, z - 1)
            if min(target) >= 0:
                pairs.append((column_device(y, z), column_device(*target)))
    return pairs


def send(value, pairs):
    return lax.ppermute(value, AXES, pairs)


def list_kernel(list_ref, count_ref, place_ref, out_ref, total_ref):
    y_in_four, y_role, z_role = place_ref[0], place_ref[1], place_ref[2]
    total = jnp.int32(0)
    for a in range(4):

        def one(k, total, a=a):
            def block(index):
                i = (index * 205) >> 11
                j = (index - 10 * i) >> 1
                return a + i, j, index & 1

            def number(x, j, l):
                return (((((j - y_in_four) & 1) ^ y_role) * 2 + (l ^ z_role)) * 4) + jnp.minimum(x, 3)

            first = block(list_ref[a, k])
            second = block(list_ref[a, 56 + k])
            mine = jnp.minimum(first[1], second[1]) == y_in_four
            one_number, two_number = number(*first), number(*second)
            one_count, two_count = count_ref[one_number], count_ref[two_number]
            swap = one_count > two_count
            sign = jnp.where(swap, -1, 1)
            left = jnp.where(swap, two_number, one_number)
            right = jnp.where(swap, one_number, two_number)
            steps = (jnp.minimum(one_count, two_count) + (GROUP - 1)) // GROUP
            word = left + right * 16 + steps * 256
            for place in range(3):
                word = word + ((sign * (first[place] - second[place]) + 1) << (13 + 2 * place))
            out_ref[total] = word
            return total + jnp.where(mine, 1, 0)

        total = lax.fori_loop(0, jnp.minimum(list_ref[a, 112], 56), one, total)
    total_ref[0] = total


def inverse_of(value):
    guess = pl.reciprocal(value, approx=True)
    return guess * (2.0 - value * guess)


def sweep_tiles(mode, list_ref, total_ref, rows_ref, columns_ref, row_sum_ref, column_sum_ref):
    forces, pulled = "F" in mode, "J" in mode
    made = 3 * forces + 4 * pulled
    lane = lax.broadcasted_iota(jnp.int32, (8, 128), 1)

    def one_pair(k, carry):
        word = list_ref[k]
        left, right, steps = word & 15, (word >> 4) & 15, (word >> 8) & 31
        offset = [(((word >> (13 + 2 * c)) & 3) - 1).astype(jnp.float32) for c in range(3)]
        weight = jnp.where(left == right, 0.5, 1.0).astype(jnp.float32)

        def row(c, scale=None, shift=None):
            value = rows_ref[right, pl.ds(c, 1), :]
            if scale is not None:
                value = value * scale
            if shift is not None:
                value = value - shift
            return jnp.broadcast_to(value, (8, 128))

        right_pos = [row(c, shift=offset[c]) for c in range(3)]
        right_charge = row(3, scale=weight)
        right_half = row(4)
        right_depth = row(5, scale=weight)
        right_cot = [row(6 + c) for c in range(3)] if pulled else None

        def one_step(step, sums):
            sums = list(sums)
            for tile in range(TILES):
                first_row = pl.multiple_of(step * GROUP + 8 * tile, 8)
                packed = columns_ref[left, pl.ds(first_row, 8), :]

                def column(c):
                    return jnp.broadcast_to(packed[:, c : c + 1], (8, 128))

                d = [column(c) - right_pos[c] for c in range(3)]
                charge = column(3)
                half = column(4) + right_half
                depth = column(5) * right_depth
                s = d[0] * d[0] + d[1] * d[1] + d[2] * d[2]
                sigma2 = half * half
                r = inverse_of(s + sigma2)
                t = sigma2 * r
                p = t * t * t
                soft = s + SOFT
                ir = lax.rsqrt(soft)
                g = jnp.exp((soft * ir) * -KAPPA) * ir
                fade = jnp.maximum(1.0 - s, 0.0)
                fade2 = fade * fade
                fr = fade * r
                kappa_term = ir + 0.5 * (ir * ir)
                h = g * (3.0 + fade * kappa_term)
                dp = depth * p
                twop = 2.0 * p - 1.0
                charges = charge * right_charge
                A = (fade2 * 8.0) * (3.0 * dp * ((p - 1.0) + fr * twop) + charges * h)
                values = []
                if forces:
                    values += [A * d[c] for c in range(3)]
                if pulled:
                    w = [column(6 + c) - right_cot[c] for c in range(3)]
                    dw = d[0] * w[0] + d[1] * w[1] + d[2] * w[2]
                    ir2 = ir * ir
                    lj = (6.0 * dp) * ((p - 1.0) + fr * (3.0 * twop + fr * (7.0 * p - 2.0)))
                    m2 = ir2 * (1.0 + 1.5 * ir + 0.75 * ir2)
                    cb = (charges * g) * (6.0 + fade * (6.0 * kappa_term + fade * m2))
                    B = (-16.0 * fade) * (lj + cb) * dw
                    values += [A * w[c] + B * d[c] for c in range(3)]
                    common = (8.0 * fade2) * h * dw
                    values += [common * right_charge]
                    last = common * charge * weight
                packed_sum = None
                for place, value in enumerate(values):
                    total = jnp.sum(value, axis=1, keepdims=True)
                    total = jnp.broadcast_to(total, (8, 128))
                    packed_sum = total if place == 0 else jnp.where(lane == place, total, packed_sum)
                here = (left, pl.ds(first_row, 8), slice(None))
                row_sum_ref[here] = row_sum_ref[here] + packed_sum
                if pulled:
                    values[-1] = -last
                sums = [a + b for a, b in zip(sums, values)]
            return tuple(sums)

        zero = jnp.zeros((8, 128), jnp.float32)
        sums = lax.fori_loop(0, steps, one_step, (zero,) * made)
        for place in range(made):
            column_sum_ref[place, right] = column_sum_ref[place, right] + sums[place]
        return carry

    lax.fori_loop(0, total_ref[0], one_pair, jnp.int32(0))


def sweep_kernel(mode, first, kick, list_ref, total_ref, *refs):
    forces, pulled = "F" in mode, "J" in mode
    made = 3 * forces + 4 * pulled
    names = ["ext"]
    if mode != "J":
        names += ["x", "v"] if not first else []
        names += [] if first else ["C", "rC", "D", "rD"]
    else:
        names += ["x", "ax", "av", "C", "rC", "D", "rD", "charge"] + (["v"] if first else [])
    outs = ["A", "B"]
    if mode == "F" and not first:
        outs += ["x_out", "v_out"]
    if mode == "FJ":
        outs += ["x_out", "v_out", "charge_out"]
    if mode == "J":
        outs += ["ax_out", "av_out", "charge_out"] + (["v_out"] if first else [])
    scratch = ["rows", "columns", "row_sum", "column_sum"]
    r = dict(zip(names + outs + scratch, refs))
    ext = r["ext"]
    inverse = ext[9]

    def received(c):
        return jnp.concatenate([r["C"][c] + r["rC"][c], r["D"][c] + r["rD"][c]], axis=0)

    position, cotangent = [], []
    for c in range(3):
        if mode != "J":
            if first:
                position.append(ext[c])
            else:
                velocity = r["v"][c] + kick * inverse * received(c)
                position.append(r["x"][c] + TIME_STEP * velocity)
                r["x_out"][c] = position[c]
                r["v_out"][c] = velocity
            if pulled:
                cotangent.append(HALF * inverse * ext[13 + c])
        else:
            if first:
                r["v_out"][c] = r["v"][c] + HALF * inverse * received(c)
            ax = r["ax"][c] + received(c + 3 if first else c)
            av = r["av"][c] + TIME_STEP * ax
            r["ax_out"][c] = ax
            r["av_out"][c] = av
            position.append(r["x"][c])
            cotangent.append(kick * inverse * av)
    _spread_and_sweep(mode, ext, position, cotangent, list_ref, total_ref, r, made, pulled)


def _spread_and_sweep(mode, ext, position, cotangent, list_ref, total_ref, r, made, pulled):
    rows = r["rows"]
    quantities = position + [ext[6], 0.5 * ext[7], ext[8]] + cotangent
    for place, value in enumerate(quantities):
        for e in range(BLOCKS):
            rows[e, place : place + 1, :] = value[e : e + 1, :]
    for e in range(BLOCKS):
        r["columns"][e, :, 0:16] = rows[e].T
        r["row_sum"][e] = jnp.zeros((128, 128), jnp.float32)
    r["column_sum"][...] = jnp.zeros(r["column_sum"].shape, jnp.float32)
    sweep_tiles(mode, list_ref, total_ref, rows, r["columns"], r["row_sum"], r["column_sum"])
    for e in range(BLOCKS):
        by_row = r["row_sum"][e].T
        target = r["A"] if (e // 4) % 2 == 0 else r["B"]
        place = (e // 8) * 4 + e % 4
        for c in range(made):
            total = by_row[c : c + 1] - jnp.sum(r["column_sum"][c, e], axis=0, keepdims=True)
            if pulled and c == made - 1:
                if mode == "J":
                    total = total + r["charge"][e : e + 1, :]
                r["charge_out"][e : e + 1, :] = total
            else:
                target[c, place : place + 1, :] = total


def sweep(mode, first, kick, plist, total, arrays):
    forces, pulled = "F" in mode, "J" in mode
    sent = 3 * forces + 3 * pulled
    made = 3 * forces + 4 * pulled
    f32 = jnp.float32
    exchange = jax.ShapeDtypeStruct((sent, 8, 128), f32)
    vector = jax.ShapeDtypeStruct((3, BLOCKS, 128), f32)
    scalar = jax.ShapeDtypeStruct((BLOCKS, 128), f32)
    outs = [exchange, exchange]
    if mode == "F" and not first:
        outs += [vector, vector]
    if mode == "FJ":
        outs += [vector, vector, scalar]
    if mode == "J":
        outs += [vector, vector, scalar] + ([vector] if first else [])
    vmem = pl.BlockSpec(memory_space=pltpu.VMEM)
    smem = pl.BlockSpec(memory_space=pltpu.SMEM)
    return pl.pallas_call(
        functools.partial(sweep_kernel, mode, first, kick),
        out_shape=outs,
        in_specs=[smem, smem] + [vmem] * len(arrays),
        out_specs=[vmem] * len(outs),
        scratch_shapes=[
            pltpu.VMEM((BLOCKS, 16, 128), f32),
            pltpu.VMEM((BLOCKS, 128, 128), f32),
            pltpu.VMEM((BLOCKS, 128, 128), f32),
            pltpu.VMEM((made, BLOCKS, 8, 128), f32),
        ],
        compiler_params=pltpu.CompilerParams(vmem_limit_bytes=32 * 1024 * 1024),
        name=f"sweep_{mode}",
    )(plist, total, *arrays)


def exchanged(A, B):
    rA, rB = send(A, swap_pairs(1, 0)), send(B, swap_pairs(1, 1))
    T0, T1 = A + rA, B + rB
    C = jnp.concatenate([T0[:, 0:4], T1[:, 0:4]], axis=1)
    D = jnp.concatenate([T0[:, 4:8], T1[:, 4:8]], axis=1)
    return C, send(C, swap_pairs(0, 0)), D, send(D, swap_pairs(0, 1))


def on_device(
    positions,
    velocities,
    charges,
    atom_types,
    atom_count,
    sigma_type,
    epsilon_type,
    masses,
    pair_list,
    pair_count,
    pos_cotangent,
    vel_cotangent,
):
    f32 = jnp.float32
    a = lax.axis_index("gx")
    y, z = column_of_device()
    y_even, z_even = y % 2 == 0, z % 2 == 0
    counts = atom_count[0, :, 0]
    alive = (lax.broadcasted_iota(jnp.int32, (4, 128), 1) < counts[:, None]).astype(f32)
    kinds = (atom_types[0, :, 0][:, None, :] == lax.broadcasted_iota(jnp.int32, (16, 1), 0)).astype(f32)
    sigma = jnp.sum(kinds * sigma_type[:, None], axis=1)
    epsilon = jnp.sum(kinds * epsilon_type[:, None], axis=1)
    listed = jnp.concatenate(
        [pair_list[0, 0, 0].reshape(112), jnp.broadcast_to(pair_count[0, 0, 0], (16,))]
    ).astype(f32)
    bundle = jnp.concatenate(
        [
            positions[0, :, 0],
            velocities[0, :, 0],
            jnp.stack(
                [charges[0, :, 0] * alive, sigma, jnp.sqrt(epsilon) * alive, 1.0 / masses[0, :, 0]], axis=1
            ),
            pos_cotangent[0, :, 0],
            vel_cotangent[0, :, 0],
            jnp.broadcast_to(counts.astype(f32)[:, None, None], (4, 1, 128)),
            jnp.broadcast_to(listed[None, None, :], (4, 1, 128)),
        ],
        axis=1,
    )
    turned = lax.dynamic_slice_in_dim(jnp.concatenate([bundle, bundle]), a, 4)
    got = [send(turned[t], spread_pairs(t)) for t in range(4)]
    stacked = jnp.stack(got[::-1])
    y_in_four = y % 4
    own = lax.dynamic_slice_in_dim(jnp.concatenate([stacked, stacked]), 3 - y_in_four, 4)
    own = jnp.swapaxes(own, 0, 1)
    lists = own[17].astype(jnp.int32)
    own = own[:17]
    upper = send(own, down_pairs(1))
    wide = jnp.where(
        z_even, jnp.concatenate([upper, own], axis=1), jnp.concatenate([own, upper], axis=1)
    )
    upper = send(wide, down_pairs(0))
    ext = jnp.where(
        y_even, jnp.concatenate([upper, wide], axis=1), jnp.concatenate([wide, upper], axis=1)
    )
    y_role, z_role = jnp.where(y_even, 1, 0), jnp.where(z_even, 1, 0)
    smem = pl.BlockSpec(memory_space=pltpu.SMEM)
    plist, total = pl.pallas_call(
        list_kernel,
        out_shape=[jax.ShapeDtypeStruct((64,), jnp.int32), jax.ShapeDtypeStruct((1,), jnp.int32)],
        in_specs=[smem] * 3,
        out_specs=[smem] * 2,
        name="keep_pairs",
    )(
        lists,
        ext[16, :, 0].astype(jnp.int32),
        jnp.stack([y_in_four, y_role, z_role]).astype(jnp.int32),
    )
    history = [ext[0:3]]
    A, B = sweep("F", True, 0.0, plist, total, [ext])
    x, v = ext[0:3], ext[3:6]
    for step in range(STEPS):
        parts = exchanged(A, B)
        kick = HALF if step == 0 else TIME_STEP
        mode = "F" if step < STEPS - 1 else "FJ"
        A, B, x, v, *rest = sweep(mode, False, kick, plist, total, [ext, x, v, *parts])
        history.append(x)
    charge = rest[0]
    ax, av = ext[10:13], ext[13:16]
    for step in range(STEPS - 1, -1, -1):
        parts = exchanged(A, B)
        first = step == STEPS - 1
        factor = TIME_STEP if step > 0 else HALF
        A, B, ax, av, charge, *rest = sweep(
            "J",
            first,
            factor,
            plist,
            total,
            [ext, history[step], ax, av, *parts, charge] + ([v] if first else []),
        )
        if first:
            v = rest[0]
    sides = charge.reshape(2, 2, 4, 128)
    A = jnp.concatenate([A, sides[:, 0].reshape(1, 8, 128)])
    B = jnp.concatenate([B, sides[:, 1].reshape(1, 8, 128)])
    C, rC, D, rD = exchanged(A, B)
    sums = jnp.concatenate([C + rC, D + rD], axis=1)
    whole = jnp.concatenate([x, v, ax + sums[:3], av, sums[3:4]])
    mine = lax.dynamic_slice_in_dim(whole, (y_role * 2 + z_role) * 4, 4, axis=1)
    mine = jnp.swapaxes(mine, 0, 1)
    turned = lax.dynamic_slice_in_dim(jnp.concatenate([mine, mine]), (y_in_four + 1) % 4, 4)
    got = [send(turned[3 - t], [(q, p) for p, q in spread_pairs(t)]) for t in range(4)]
    stacked = jnp.stack(got)
    out = lax.dynamic_slice_in_dim(jnp.concatenate([stacked, stacked]), (4 - a) % 4, 4)
    out = out[None, :, None]
    return (
        out[:, :, :, 0:3],
        out[:, :, :, 3:6],
        out[:, :, :, 6:9],
        out[:, :, :, 9:12],
        out[:, :, :, 12] * alive[None, :, None],
    )


def solution(mesh):
    vector = P("gx", "gy", "gz", None, None)
    scalar = P("gx", "gy", "gz", None)
    block = P("gx", "gy", "gz")
    in_specs = (
        vector, vector, scalar, scalar, block, P(), P(), scalar, vector, block, vector, vector,
    )
    out_specs = (vector, vector, vector, vector, scalar)
    return jax.shard_map(on_device, mesh=mesh, in_specs=in_specs, out_specs=out_specs, check_vma=False)
```

```python
import functools

import jax
import jax.numpy as jnp
from jax import lax
from jax.experimental import pallas as pl
from jax.experimental.pallas import tpu as pltpu
from jax.sharding import PartitionSpec as P

STEPS = 5
SOFT = 0.04
KAPPA = 2.0
COULOMB = 4.0
TIME_STEP = 0.004
HALF = 0.5 * TIME_STEP
AXES = ("gx", "gy", "gz")
GRID = 16
BLOCKS = 16
ROWS = 18
TILES = 4
GROUP = 8 * TILES
JOBS = 2
LIST = 56 * (128 // GROUP) + 16


def column_device(y, z):
    phys_y = y // 4
    phys_x = y % 4 if phys_y % 2 == 0 else 3 - y % 4
    phys_z = z // 2
    core = z % 2 if phys_z % 2 == 0 else 1 - z % 2
    return (phys_y * 4 + (phys_z % 2) * 2 + core) * 16 + (phys_z // 2) * 4 + phys_x


def column_of_device():
    gx, gy, gz = (lax.axis_index(name) for name in AXES)
    low, core = gy // 2, gy % 2
    high, phys_x = gz // 4, gz % 4
    phys_z = high * 2 + low
    y = gx * 4 + jnp.where(gx % 2 == 0, phys_x, 3 - phys_x)
    z = phys_z * 2 + jnp.where(phys_z % 2 == 0, core, 1 - core)
    return y, z


def spread_pairs(turn):
    return [
        ((a * 4 + b) * 16 + c, column_device(4 * b + (a + turn) % 4, c))
        for a in range(4)
        for b in range(4)
        for c in range(16)
    ]


def swap_pairs(axis, parity):
    pairs = []
    for y in range(GRID):
        for z in range(GRID):
            own = (y, z)[axis]
            other = own + 1 if own % 2 == parity else own - 1
            if 0 <= other < GRID:
                target = (other, z) if axis == 0 else (y, other)
                pairs.append((column_device(y, z), column_device(*target)))
    return pairs


def down_pairs(axis):
    pairs = []
    for y in range(GRID):
        for z in range(GRID):
            target = (y - 1, z) if axis == 0 else (y, z - 1)
            if min(target) >= 0:
                pairs.append((column_device(y, z), column_device(*target)))
    return pairs


def send(value, pairs):
    return lax.ppermute(value, AXES, pairs)


def list_kernel(list_ref, count_ref, place_ref, out_ref, total_ref):
    y_in_four, y_role, z_role = place_ref[0], place_ref[1], place_ref[2]
    total = jnp.int32(0)
    for a in range(4):

        def one(k, total, a=a):
            def block(index):
                i = (index * 205) >> 11
                j = (index - 10 * i) >> 1
                return a + i, j, index & 1

            def number(x, j, l):
                return (((((j - y_in_four) & 1) ^ y_role) * 2 + (l ^ z_role)) * 4) + jnp.minimum(x, 3)

            first = block(list_ref[a, k])
            second = block(list_ref[a, 56 + k])
            mine = jnp.minimum(first[1], second[1]) == y_in_four
            one_number, two_number = number(*first), number(*second)
            one_count, two_count = count_ref[one_number], count_ref[two_number]
            swap = one_count > two_count
            sign = jnp.where(swap, -1, 1)
            left = jnp.where(swap, two_number, one_number)
            right = jnp.where(swap, one_number, two_number)
            steps = (jnp.minimum(one_count, two_count) + (GROUP - 1)) // GROUP
            word = left + right * 16 + (jnp.where(left == right, 1, 2) << 18)
            for place in range(3):
                word = word + ((sign * (first[place] - second[place]) + 1) << (12 + 2 * place))
            for step in range(128 // GROUP):
                out_ref[total + step] = word + step * 256
            return total + jnp.where(mine, steps, 0)

        total = lax.fori_loop(0, jnp.minimum(list_ref[a, 112], 56), one, total)
    for job in range(JOBS):
        out_ref[total + job] = 0
    total_ref[0] = (total + JOBS - 1) // JOBS


def inverse_of(value):
    guess = pl.reciprocal(value, approx=True)
    return guess * (2.0 - value * guess)


def sweep_tiles(mode, list_ref, total_ref, rows_ref, columns_ref, row_sum_ref, column_sum_ref):
    forces, pulled = "F" in mode, "J" in mode
    made = 3 * forces + 4 * pulled

    def one_job(word):
        left, right, step = word & 15, (word >> 4) & 15, (word >> 8) & 15
        offset = [(((word >> (12 + 2 * c)) & 3) - 1).astype(jnp.float32) for c in range(3)]
        weight = (word >> 18).astype(jnp.float32) * 0.5

        def row(c, scale=None, shift=None):
            value = rows_ref[c, pl.ds(right, 1), :]
            if scale is not None:
                value = value * scale
            if shift is not None:
                value = value - shift
            return jnp.broadcast_to(value, (8, 128))

        right_pos = [row(c, shift=offset[c]) for c in range(3)]
        right_charge = row(3, scale=weight)
        right_half = row(4)
        right_depth = row(5, scale=weight)
        right_cot = [row(6 + c) for c in range(3)] if pulled else None

        sums = None
        for tile in range(TILES):
            eight = pl.ds(pl.multiple_of(left * 128 + step * GROUP + 8 * tile, 8), 8)

            def column(c):
                return columns_ref[c, eight, :]

            d = [column(c) - right_pos[c] for c in range(3)]
            charge = column(3)
            half = column(4) + right_half
            depth = column(5) * right_depth
            s = d[0] * d[0] + d[1] * d[1] + d[2] * d[2]
            sigma2 = half * half
            r = inverse_of(s + sigma2)
            t = sigma2 * r
            p = t * t * t
            soft = s + SOFT
            ir = lax.rsqrt(soft)
            g = jnp.exp((soft * ir) * -KAPPA) * ir
            fade = jnp.maximum(1.0 - s, 0.0)
            fade2 = fade * fade
            fr = fade * r
            kappa_term = ir + 0.5 * (ir * ir)
            h = g * (3.0 + fade * kappa_term)
            dp = depth * p
            twop = 2.0 * p - 1.0
            charges = charge * right_charge
            A = (fade2 * 8.0) * (3.0 * dp * ((p - 1.0) + fr * twop) + charges * h)
            values = []
            if forces:
                values += [A * d[c] for c in range(3)]
            if pulled:
                w = [column(6 + c) - right_cot[c] for c in range(3)]
                dw = d[0] * w[0] + d[1] * w[1] + d[2] * w[2]
                ir2 = ir * ir
                lj = (6.0 * dp) * ((p - 1.0) + fr * (3.0 * twop + fr * (7.0 * p - 2.0)))
                m2 = ir2 * (1.0 + 1.5 * ir + 0.75 * ir2)
                cb = (charges * g) * (6.0 + fade * (6.0 * kappa_term + fade * m2))
                B = (-16.0 * fade) * (lj + cb) * dw
                values += [A * w[c] + B * d[c] for c in range(3)]
                common = (8.0 * fade2) * h * dw
                values += [common * right_charge]
                last = common * charge * weight
            for place, value in enumerate(values):
                row_sum_ref[place, eight, :] = row_sum_ref[place, eight, :] + value
            if pulled:
                values[-1] = -last
            sums = values if sums is None else [a + b for a, b in zip(sums, values)]
        for place in range(made):
            column_sum_ref[place, right] = column_sum_ref[place, right] + sums[place]

    def one_step(k, carry):
        for job in range(JOBS):
            one_job(list_ref[k * JOBS + job])
        return carry

    lax.fori_loop(0, total_ref[0], one_step, jnp.int32(0))


def sweep_kernel(mode, first, kick, list_ref, total_ref, *refs):
    forces, pulled = "F" in mode, "J" in mode
    made = 3 * forces + 4 * pulled
    names = ["ext"]
    if mode != "J":
        names += ["x", "v"] if not first else []
        names += [] if first else ["C", "rC", "D", "rD"]
    else:
        names += ["x", "ax", "av", "C", "rC", "D", "rD", "charge"] + (["v"] if first else [])
    outs = ["A", "B"]
    if mode == "F" and not first:
        outs += ["x_out", "v_out"]
    if mode == "FJ":
        outs += ["x_out", "v_out", "charge_out"]
    if mode == "J":
        outs += ["ax_out", "av_out", "charge_out"] + (["v_out"] if first else [])
    scratch = ["rows", "columns", "row_sum", "column_sum"]
    r = dict(zip(names + outs + scratch, refs))
    ext = r["ext"]
    inverse = ext[9]

    def received(c):
        return jnp.concatenate([r["C"][c] + r["rC"][c], r["D"][c] + r["rD"][c]], axis=0)

    position, cotangent = [], []
    for c in range(3):
        if mode != "J":
            if first:
                position.append(ext[c])
            else:
                velocity = r["v"][c] + kick * inverse * received(c)
                position.append(r["x"][c] + TIME_STEP * velocity)
                r["x_out"][c] = position[c]
                r["v_out"][c] = velocity
            if pulled:
                cotangent.append(HALF * inverse * ext[13 + c])
        else:
            if first:
                r["v_out"][c] = r["v"][c] + HALF * inverse * received(c)
            ax = r["ax"][c] + received(c + 3 if first else c)
            av = r["av"][c] + TIME_STEP * ax
            r["ax_out"][c] = ax
            r["av_out"][c] = av
            position.append(r["x"][c])
            cotangent.append(kick * inverse * av)
    _spread_and_sweep(mode, ext, position, cotangent, list_ref, total_ref, r, made, pulled)


def _spread_and_sweep(mode, ext, position, cotangent, list_ref, total_ref, r, made, pulled):
    rows = r["rows"]
    quantities = position + [ext[6], 0.5 * ext[7], ext[8]] + cotangent
    for place, value in enumerate(quantities):
        rows[place] = value
        turned = value.T
        for e in range(BLOCKS):
            r["columns"][place, e * 128 : (e + 1) * 128, :] = jnp.broadcast_to(turned[:, e : e + 1], (128, 128))
    r["row_sum"][...] = jnp.zeros(r["row_sum"].shape, jnp.float32)
    r["column_sum"][...] = jnp.zeros(r["column_sum"].shape, jnp.float32)
    sweep_tiles(mode, list_ref, total_ref, rows, r["columns"], r["row_sum"], r["column_sum"])
    lane = lax.broadcasted_iota(jnp.int32, (128, BLOCKS), 1)
    for c in range(made):
        by_atom = jnp.zeros((128, BLOCKS), jnp.float32)
        for e in range(BLOCKS):
            total = jnp.sum(r["row_sum"][c, e * 128 : (e + 1) * 128, :], axis=1, keepdims=True)
            by_atom = jnp.where(lane == e, jnp.broadcast_to(total, (128, BLOCKS)), by_atom)
        total = by_atom.T - jnp.sum(r["column_sum"][c], axis=1)
        if pulled and c == made - 1:
            if mode == "J":
                total = total + r["charge"][...]
            r["charge_out"][...] = total
        else:
            r["A"][c] = jnp.concatenate([total[0:4], total[8:12]], axis=0)
            r["B"][c] = jnp.concatenate([total[4:8], total[12:16]], axis=0)


def sweep(mode, first, kick, plist, total, arrays):
    forces, pulled = "F" in mode, "J" in mode
    sent = 3 * forces + 3 * pulled
    made = 3 * forces + 4 * pulled
    quantities = 6 + 3 * pulled
    f32 = jnp.float32
    exchange = jax.ShapeDtypeStruct((sent, 8, 128), f32)
    vector = jax.ShapeDtypeStruct((3, BLOCKS, 128), f32)
    scalar = jax.ShapeDtypeStruct((BLOCKS, 128), f32)
    outs = [exchange, exchange]
    if mode == "F" and not first:
        outs += [vector, vector]
    if mode == "FJ":
        outs += [vector, vector, scalar]
    if mode == "J":
        outs += [vector, vector, scalar] + ([vector] if first else [])
    vmem = pl.BlockSpec(memory_space=pltpu.VMEM)
    smem = pl.BlockSpec(memory_space=pltpu.SMEM)
    return pl.pallas_call(
        functools.partial(sweep_kernel, mode, first, kick),
        out_shape=outs,
        in_specs=[smem, smem] + [vmem] * len(arrays),
        out_specs=[vmem] * len(outs),
        scratch_shapes=[
            pltpu.VMEM((quantities, BLOCKS, 128), f32),
            pltpu.VMEM((quantities, BLOCKS * 128, 128), f32),
            pltpu.VMEM((made, BLOCKS * 128, 128), f32),
            pltpu.VMEM((made, BLOCKS, 8, 128), f32),
        ],
        compiler_params=pltpu.CompilerParams(vmem_limit_bytes=32 * 1024 * 1024),
        name=f"sweep_{mode}",
    )(plist, total, *arrays)


def exchanged(A, B):
    rA, rB = send(A, swap_pairs(1, 0)), send(B, swap_pairs(1, 1))
    T0, T1 = A + rA, B + rB
    C = jnp.concatenate([T0[:, 0:4], T1[:, 0:4]], axis=1)
    D = jnp.concatenate([T0[:, 4:8], T1[:, 4:8]], axis=1)
    return C, send(C, swap_pairs(0, 0)), D, send(D, swap_pairs(0, 1))


def on_device(
    positions,
    velocities,
    charges,
    atom_types,
    atom_count,
    sigma_type,
    epsilon_type,
    masses,
    pair_list,
    pair_count,
    pos_cotangent,
    vel_cotangent,
):
    f32 = jnp.float32
    a = lax.axis_index("gx")
    y, z = column_of_device()
    y_even, z_even = y % 2 == 0, z % 2 == 0
    counts = atom_count[0, :, 0]
    alive = (lax.broadcasted_iota(jnp.int32, (4, 128), 1) < counts[:, None]).astype(f32)
    kinds = (atom_types[0, :, 0][:, None, :] == lax.broadcasted_iota(jnp.int32, (16, 1), 0)).astype(f32)
    sigma = jnp.sum(kinds * sigma_type[:, None], axis=1)
    epsilon = jnp.sum(kinds * epsilon_type[:, None], axis=1)
    listed = jnp.concatenate(
        [pair_list[0, 0, 0].reshape(112), jnp.broadcast_to(pair_count[0, 0, 0], (16,))]
    ).astype(f32)
    bundle = jnp.concatenate(
        [
            positions[0, :, 0],
            velocities[0, :, 0],
            jnp.stack(
                [charges[0, :, 0] * alive, sigma, jnp.sqrt(epsilon) * alive, 1.0 / masses[0, :, 0]], axis=1
            ),
            pos_cotangent[0, :, 0],
            vel_cotangent[0, :, 0],
            jnp.broadcast_to(counts.astype(f32)[:, None, None], (4, 1, 128)),
            jnp.broadcast_to(listed[None, None, :], (4, 1, 128)),
        ],
        axis=1,
    )
    turned = lax.dynamic_slice_in_dim(jnp.concatenate([bundle, bundle]), a, 4)
    got = [send(turned[t], spread_pairs(t)) for t in range(4)]
    stacked = jnp.stack(got[::-1])
    y_in_four = y % 4
    own = lax.dynamic_slice_in_dim(jnp.concatenate([stacked, stacked]), 3 - y_in_four, 4)
    own = jnp.swapaxes(own, 0, 1)
    lists = own[17].astype(jnp.int32)
    own = own[:17]
    upper = send(own, down_pairs(1))
    wide = jnp.where(
        z_even, jnp.concatenate([upper, own], axis=1), jnp.concatenate([own, upper], axis=1)
    )
    upper = send(wide, down_pairs(0))
    ext = jnp.where(
        y_even, jnp.concatenate([upper, wide], axis=1), jnp.concatenate([wide, upper], axis=1)
    )
    y_role, z_role = jnp.where(y_even, 1, 0), jnp.where(z_even, 1, 0)
    smem = pl.BlockSpec(memory_space=pltpu.SMEM)
    plist, total = pl.pallas_call(
        list_kernel,
        out_shape=[jax.ShapeDtypeStruct((LIST,), jnp.int32), jax.ShapeDtypeStruct((1,), jnp.int32)],
        in_specs=[smem] * 3,
        out_specs=[smem] * 2,
        name="keep_pairs",
    )(
        lists,
        ext[16, :, 0].astype(jnp.int32),
        jnp.stack([y_in_four, y_role, z_role]).astype(jnp.int32),
    )
    history = [ext[0:3]]
    A, B = sweep("F", True, 0.0, plist, total, [ext])
    x, v = ext[0:3], ext[3:6]
    for step in range(STEPS):
        parts = exchanged(A, B)
        kick = HALF if step == 0 else TIME_STEP
        mode = "F" if step < STEPS - 1 else "FJ"
        A, B, x, v, *rest = sweep(mode, False, kick, plist, total, [ext, x, v, *parts])
        history.append(x)
    charge = rest[0]
    ax, av = ext[10:13], ext[13:16]
    for step in range(STEPS - 1, -1, -1):
        parts = exchanged(A, B)
        first = step == STEPS - 1
        factor = TIME_STEP if step > 0 else HALF
        A, B, ax, av, charge, *rest = sweep(
            "J",
            first,
            factor,
            plist,
            total,
            [ext, history[step], ax, av, *parts, charge] + ([v] if first else []),
        )
        if first:
            v = rest[0]
    sides = charge.reshape(2, 2, 4, 128)
    A = jnp.concatenate([A, sides[:, 0].reshape(1, 8, 128)])
    B = jnp.concatenate([B, sides[:, 1].reshape(1, 8, 128)])
    C, rC, D, rD = exchanged(A, B)
    sums = jnp.concatenate([C + rC, D + rD], axis=1)
    whole = jnp.concatenate([x, v, ax + sums[:3], av, sums[3:4]])
    mine = lax.dynamic_slice_in_dim(whole, (y_role * 2 + z_role) * 4, 4, axis=1)
    mine = jnp.swapaxes(mine, 0, 1)
    turned = lax.dynamic_slice_in_dim(jnp.concatenate([mine, mine]), (y_in_four + 1) % 4, 4)
    got = [send(turned[3 - t], [(q, p) for p, q in spread_pairs(t)]) for t in range(4)]
    stacked = jnp.stack(got)
    out = lax.dynamic_slice_in_dim(jnp.concatenate([stacked, stacked]), (4 - a) % 4, 4)
    out = out[None, :, None]
    return (
        out[:, :, :, 0:3],
        out[:, :, :, 3:6],
        out[:, :, :, 6:9],
        out[:, :, :, 9:12],
        out[:, :, :, 12] * alive[None, :, None],
    )


def solution(mesh):
    vector = P("gx", "gy", "gz", None, None)
    scalar = P("gx", "gy", "gz", None)
    block = P("gx", "gy", "gz")
    in_specs = (
        vector, vector, scalar, scalar, block, P(), P(), scalar, vector, block, vector, vector,
    )
    out_specs = (vector, vector, vector, vector, scalar)
    return jax.shard_map(on_device, mesh=mesh, in_specs=in_specs, out_specs=out_specs, check_vma=False)
```

```python
import functools

import jax
import jax.numpy as jnp
from jax import lax
from jax.experimental import pallas as pl
from jax.experimental.pallas import tpu as pltpu
from jax.sharding import PartitionSpec as P

STEPS = 5
SOFT = 0.04
KAPPA = 2.0
LOG2E = 1.4426950408889634
COULOMB = 4.0
TIME_STEP = 0.004
HALF = 0.5 * TIME_STEP
AXES = ("gx", "gy", "gz")
GRID = 16
OWN = 8
BLOCKS = 16
ROWS = 18
TILES = 4
GROUP = 8 * TILES
JOBS = 3
LIST = 56 * (128 // GROUP) + 16


def column_device(y, z):
    phys_y = y // 4
    phys_x = y % 4 if phys_y % 2 == 0 else 3 - y % 4
    phys_z = z // 2
    core = z % 2 if phys_z % 2 == 0 else 1 - z % 2
    return (phys_y * 4 + (phys_z % 2) * 2 + core) * 16 + (phys_z // 2) * 4 + phys_x


def column_of_device():
    gx, gy, gz = (lax.axis_index(name) for name in AXES)
    low, core = gy // 2, gy % 2
    high, phys_x = gz // 4, gz % 4
    phys_z = high * 2 + low
    y = gx * 4 + jnp.where(gx % 2 == 0, phys_x, 3 - phys_x)
    z = phys_z * 2 + jnp.where(phys_z % 2 == 0, core, 1 - core)
    return y, z


def spread_pairs(turn):
    return [
        ((a * 4 + b) * 16 + c, column_device(4 * b + (a + turn) % 4, c))
        for a in range(4)
        for b in range(4)
        for c in range(16)
    ]


def swap_pairs(axis, parity):
    pairs = []
    for y in range(GRID):
        for z in range(GRID):
            own = (y, z)[axis]
            other = own + 1 if own % 2 == parity else own - 1
            if 0 <= other < GRID:
                target = (other, z) if axis == 0 else (y, other)
                pairs.append((column_device(y, z), column_device(*target)))
    return pairs


def down_pairs(axis):
    pairs = []
    for y in range(GRID):
        for z in range(GRID):
            target = (y - 1, z) if axis == 0 else (y, z - 1)
            if min(target) >= 0:
                pairs.append((column_device(y, z), column_device(*target)))
    return pairs


def send(value, pairs):
    return lax.ppermute(value, AXES, pairs)


def list_kernel(list_ref, count_ref, place_ref, out_ref, total_ref):
    y_in_four, y_role, z_role = place_ref[0], place_ref[1], place_ref[2]
    total = jnp.int32(0)
    for a in range(4):

        def one(k, total, a=a):
            def block(index):
                i = (index * 205) >> 11
                j = (index - 10 * i) >> 1
                return a + i, j, index & 1

            def number(x, j, l):
                return (((((j - y_in_four) & 1) ^ y_role) * 2 + (l ^ z_role)) * 4) + jnp.minimum(x, 3)

            first = block(list_ref[a, k])
            second = block(list_ref[a, 56 + k])
            mine = jnp.minimum(first[1], second[1]) == y_in_four
            one_number, two_number = number(*first), number(*second)
            one_count, two_count = count_ref[one_number], count_ref[two_number]
            swap = (first[2] > second[2]) | ((first[2] == second[2]) & (one_count > two_count))
            sign = jnp.where(swap, -1, 1)
            left = jnp.where(swap, two_number, one_number)
            right = jnp.where(swap, one_number, two_number)
            steps = (jnp.where(swap, two_count, one_count) + (GROUP - 1)) // GROUP
            own_left = ((left >> 3) << 2) + (left & 3)
            word = own_left + right * 16 + (jnp.where(left == right, 1, 2) << 18)
            for place in range(3):
                word = word + ((sign * (first[place] - second[place]) + 1) << (12 + 2 * place))
            for step in range(128 // GROUP):
                out_ref[total + step] = word + step * 256
            return total + jnp.where(mine, steps, 0)

        total = lax.fori_loop(0, jnp.minimum(list_ref[a, 112], 56), one, total)
    for job in range(JOBS):
        out_ref[total + job] = 0
    total_ref[0] = (total + JOBS - 1) // JOBS
    total_ref[1] = z_role


def inverse_of(value):
    guess = pl.reciprocal(value, approx=True)
    return guess * (2.0 - value * guess)


def sweep_tiles(mode, list_ref, total_ref, rows_ref, columns_ref, row_sum_ref, column_sum_ref):
    forces, pulled = "F" in mode, "J" in mode
    made = 3 * forces + 4 * pulled

    def one_job(word):
        left, right, step = word & 15, (word >> 4) & 15, (word >> 8) & 15
        offset = [(((word >> (12 + 2 * c)) & 3) - 1).astype(jnp.float32) for c in range(3)]
        weight = (word >> 18).astype(jnp.float32) * 0.5

        def row(c, scale=None, shift=None):
            value = rows_ref[c, pl.ds(right, 1), :]
            if scale is not None:
                value = value * scale
            if shift is not None:
                value = value - shift
            return jnp.broadcast_to(value, (8, 128))

        right_pos = [row(c, shift=offset[c]) for c in range(3)]
        right_charge = row(3, scale=8.0 * weight)
        right_half = row(4)
        right_depth = row(5, scale=24.0 * weight)
        right_cot = [row(6 + c) for c in range(3)] if pulled else None

        sums = None
        for tile in range(TILES):
            eight = pl.ds(pl.multiple_of(left * 128 + step * GROUP + 8 * tile, 8), 8)

            def column(c):
                return columns_ref[c, eight, :]

            d = [column(c) - right_pos[c] for c in range(3)]
            charge = column(3)
            half = column(4) + right_half
            depth = column(5) * right_depth
            s = d[0] * d[0] + d[1] * d[1] + d[2] * d[2]
            sigma2 = half * half
            r = inverse_of(s + sigma2)
            t = sigma2 * r
            p = t * t * t
            soft = s + SOFT
            ir = lax.rsqrt(soft)
            g = jnp.exp2((soft * ir) * (-KAPPA * LOG2E)) * ir
            fade = jnp.maximum(1.0 - s, 0.0)
            fade2 = fade * fade
            fr = fade * r
            ir2 = ir * ir
            fade_kappa = fade * (ir + 0.5 * ir2)
            fade2h = fade2 * (g * (3.0 + fade_kappa))
            dp = depth * p
            charges = charge * right_charge
            A = (fade2 * dp) * ((p - 1.0) + fr * (2.0 * p - 1.0)) + charges * fade2h
            values = []
            if forces:
                values += [A * d[c] for c in range(3)]
            if pulled:
                w = [column(6 + c) - right_cot[c] for c in range(3)]
                dw = d[0] * w[0] + d[1] * w[1] + d[2] * w[2]
                lj = (2.0 * p - 2.0) + fr * ((12.0 * p - 6.0) + fr * (14.0 * p - 4.0))
                m2 = ir2 * (1.0 + 1.5 * ir + 0.75 * ir2)
                coulomb = 6.0 * (1.0 + fade_kappa) + fade2 * m2
                B = (-2.0 * fade) * (dp * lj + (charges * g) * coulomb) * dw
                values += [A * w[c] + B * d[c] for c in range(3)]
                common = fade2h * dw
                values += [common * right_charge]
                last = common * charge
            for place, value in enumerate(values):
                row_sum_ref[place, eight, :] = row_sum_ref[place, eight, :] + value
            if pulled:
                values[-1] = -last
            sums = values if sums is None else [a + b for a, b in zip(sums, values)]
        if pulled:
            sums[-1] = sums[-1] * (8.0 * weight)
        for place in range(made):
            column_sum_ref[place, right] = column_sum_ref[place, right] + sums[place]

    def one_step(k, carry):
        for job in range(JOBS):
            one_job(list_ref[k * JOBS + job])
        return carry

    lax.fori_loop(0, total_ref[0], one_step, jnp.int32(0))


def sweep_kernel(mode, first, kick, list_ref, total_ref, *refs):
    forces, pulled = "F" in mode, "J" in mode
    made = 3 * forces + 4 * pulled
    names = ["ext"]
    if mode != "J":
        names += ["x", "v"] if not first else []
        names += [] if first else ["C", "rC", "D", "rD"]
    else:
        names += ["x", "ax", "av", "C", "rC", "D", "rD", "charge"] + (["v"] if first else [])
    outs = ["A", "B"]
    if mode == "F" and not first:
        outs += ["x_out", "v_out"]
    if mode == "FJ":
        outs += ["x_out", "v_out", "charge_out"]
    if mode == "J":
        outs += ["ax_out", "av_out", "charge_out"] + (["v_out"] if first else [])
    scratch = ["rows", "columns", "row_sum", "column_sum"]
    r = dict(zip(names + outs + scratch, refs))
    ext = r["ext"]
    inverse = ext[9]

    def received(c):
        return jnp.concatenate([r["C"][c] + r["rC"][c], r["D"][c] + r["rD"][c]], axis=0)

    position, cotangent = [], []
    for c in range(3):
        if mode != "J":
            if first:
                position.append(ext[c])
            else:
                velocity = r["v"][c] + kick * inverse * received(c)
                position.append(r["x"][c] + TIME_STEP * velocity)
                r["x_out"][c] = position[c]
                r["v_out"][c] = velocity
            if pulled:
                cotangent.append(HALF * inverse * ext[13 + c])
        else:
            if first:
                r["v_out"][c] = r["v"][c] + HALF * inverse * received(c)
            ax = r["ax"][c] + received(c + 3 if first else c)
            av = r["av"][c] + TIME_STEP * ax
            r["ax_out"][c] = ax
            r["av_out"][c] = av
            position.append(r["x"][c])
            cotangent.append(kick * inverse * av)
    _spread_and_sweep(mode, ext, position, cotangent, list_ref, total_ref, r, made, pulled)


def _spread_and_sweep(mode, ext, position, cotangent, list_ref, total_ref, r, made, pulled):
    rows = r["rows"]
    own_first = total_ref[1] == 0
    quantities = position + [ext[6], 0.5 * ext[7], ext[8]] + cotangent
    for place, value in enumerate(quantities):
        rows[place] = value
        near = jnp.concatenate([value[0:4], value[8:12]], axis=0)
        far = jnp.concatenate([value[4:8], value[12:16]], axis=0)
        turned = jnp.where(own_first, near, far).T
        for e in range(OWN):
            r["columns"][place, e * 128 : (e + 1) * 128, :] = jnp.broadcast_to(turned[:, e : e + 1], (128, 128))
    r["row_sum"][...] = jnp.zeros(r["row_sum"].shape, jnp.float32)
    r["column_sum"][...] = jnp.zeros(r["column_sum"].shape, jnp.float32)
    sweep_tiles(mode, list_ref, total_ref, rows, r["columns"], r["row_sum"], r["column_sum"])
    lane = lax.broadcasted_iota(jnp.int32, (128, OWN), 1)
    for c in range(made):
        by_atom = jnp.zeros((128, OWN), jnp.float32)
        for e in range(OWN):
            total = jnp.sum(r["row_sum"][c, e * 128 : (e + 1) * 128, :], axis=1, keepdims=True)
            by_atom = jnp.where(lane == e, jnp.broadcast_to(total, (128, OWN)), by_atom)
        own = by_atom.T
        others = jnp.sum(r["column_sum"][c], axis=1)
        A = jnp.where(own_first, own, 0.0) - jnp.concatenate([others[0:4], others[8:12]], axis=0)
        B = jnp.where(own_first, 0.0, own) - jnp.concatenate([others[4:8], others[12:16]], axis=0)
        if pulled and c == made - 1:
            total = jnp.concatenate([A[0:4], B[0:4], A[4:8], B[4:8]], axis=0)
            if mode == "J":
                total = total + r["charge"][...]
            r["charge_out"][...] = total
        else:
            r["A"][c] = A
            r["B"][c] = B


def sweep(mode, first, kick, plist, total, arrays):
    forces, pulled = "F" in mode, "J" in mode
    sent = 3 * forces + 3 * pulled
    made = 3 * forces + 4 * pulled
    quantities = 6 + 3 * pulled
    f32 = jnp.float32
    exchange = jax.ShapeDtypeStruct((sent, 8, 128), f32)
    vector = jax.ShapeDtypeStruct((3, BLOCKS, 128), f32)
    scalar = jax.ShapeDtypeStruct((BLOCKS, 128), f32)
    outs = [exchange, exchange]
    if mode == "F" and not first:
        outs += [vector, vector]
    if mode == "FJ":
        outs += [vector, vector, scalar]
    if mode == "J":
        outs += [vector, vector, scalar] + ([vector] if first else [])
    vmem = pl.BlockSpec(memory_space=pltpu.VMEM)
    smem = pl.BlockSpec(memory_space=pltpu.SMEM)
    return pl.pallas_call(
        functools.partial(sweep_kernel, mode, first, kick),
        out_shape=outs,
        in_specs=[smem, smem] + [vmem] * len(arrays),
        out_specs=[vmem] * len(outs),
        scratch_shapes=[
            pltpu.VMEM((quantities, BLOCKS, 128), f32),
            pltpu.VMEM((quantities, OWN * 128, 128), f32),
            pltpu.VMEM((made, OWN * 128, 128), f32),
            pltpu.VMEM((made, BLOCKS, 8, 128), f32),
        ],
        compiler_params=pltpu.CompilerParams(vmem_limit_bytes=32 * 1024 * 1024),
        name=f"sweep_{mode}",
    )(plist, total, *arrays)


def exchanged(A, B):
    rA, rB = send(A, swap_pairs(1, 0)), send(B, swap_pairs(1, 1))
    T0, T1 = A + rA, B + rB
    C = jnp.concatenate([T0[:, 0:4], T1[:, 0:4]], axis=1)
    D = jnp.concatenate([T0[:, 4:8], T1[:, 4:8]], axis=1)
    return C, send(C, swap_pairs(0, 0)), D, send(D, swap_pairs(0, 1))


def on_device(
    positions,
    velocities,
    charges,
    atom_types,
    atom_count,
    sigma_type,
    epsilon_type,
    masses,
    pair_list,
    pair_count,
    pos_cotangent,
    vel_cotangent,
):
    f32 = jnp.float32
    a = lax.axis_index("gx")
    y, z = column_of_device()
    y_even, z_even = y % 2 == 0, z % 2 == 0
    counts = atom_count[0, :, 0]
    alive = (lax.broadcasted_iota(jnp.int32, (4, 128), 1) < counts[:, None]).astype(f32)
    kinds = (atom_types[0, :, 0][:, None, :] == lax.broadcasted_iota(jnp.int32, (16, 1), 0)).astype(f32)
    sigma = jnp.sum(kinds * sigma_type[:, None], axis=1)
    epsilon = jnp.sum(kinds * epsilon_type[:, None], axis=1)
    listed = jnp.concatenate(
        [pair_list[0, 0, 0].reshape(112), jnp.broadcast_to(pair_count[0, 0, 0], (16,))]
    ).astype(f32)
    bundle = jnp.concatenate(
        [
            positions[0, :, 0],
            velocities[0, :, 0],
            jnp.stack(
                [charges[0, :, 0] * alive, sigma, jnp.sqrt(epsilon) * alive, 1.0 / masses[0, :, 0]], axis=1
            ),
            pos_cotangent[0, :, 0],
            vel_cotangent[0, :, 0],
            jnp.broadcast_to(counts.astype(f32)[:, None, None], (4, 1, 128)),
            jnp.broadcast_to(listed[None, None, :], (4, 1, 128)),
        ],
        axis=1,
    )
    turned = lax.dynamic_slice_in_dim(jnp.concatenate([bundle, bundle]), a, 4)
    got = [send(turned[t], spread_pairs(t)) for t in range(4)]
    stacked = jnp.stack(got[::-1])
    y_in_four = y % 4
    own = lax.dynamic_slice_in_dim(jnp.concatenate([stacked, stacked]), 3 - y_in_four, 4)
    own = jnp.swapaxes(own, 0, 1)
    lists = own[17].astype(jnp.int32)
    own = own[:17]
    upper = send(own, down_pairs(1))
    wide = jnp.where(
        z_even, jnp.concatenate([upper, own], axis=1), jnp.concatenate([own, upper], axis=1)
    )
    upper = send(wide, down_pairs(0))
    ext = jnp.where(
        y_even, jnp.concatenate([upper, wide], axis=1), jnp.concatenate([wide, upper], axis=1)
    )
    y_role, z_role = jnp.where(y_even, 1, 0), jnp.where(z_even, 1, 0)
    smem = pl.BlockSpec(memory_space=pltpu.SMEM)
    plist, total = pl.pallas_call(
        list_kernel,
        out_shape=[jax.ShapeDtypeStruct((LIST,), jnp.int32), jax.ShapeDtypeStruct((2,), jnp.int32)],
        in_specs=[smem] * 3,
        out_specs=[smem] * 2,
        name="keep_pairs",
    )(
        lists,
        ext[16, :, 0].astype(jnp.int32),
        jnp.stack([y_in_four, y_role, z_role]).astype(jnp.int32),
    )
    history = [ext[0:3]]
    A, B = sweep("F", True, 0.0, plist, total, [ext])
    x, v = ext[0:3], ext[3:6]
    for step in range(STEPS):
        parts = exchanged(A, B)
        kick = HALF if step == 0 else TIME_STEP
        mode = "F" if step < STEPS - 1 else "FJ"
        A, B, x, v, *rest = sweep(mode, False, kick, plist, total, [ext, x, v, *parts])
        history.append(x)
    charge = rest[0]
    ax, av = ext[10:13], ext[13:16]
    for step in range(STEPS - 1, -1, -1):
        parts = exchanged(A, B)
        first = step == STEPS - 1
        factor = TIME_STEP if step > 0 else HALF
        A, B, ax, av, charge, *rest = sweep(
            "J",
            first,
            factor,
            plist,
            total,
            [ext, history[step], ax, av, *parts, charge] + ([v] if first else []),
        )
        if first:
            v = rest[0]
    sides = charge.reshape(2, 2, 4, 128)
    A = jnp.concatenate([A, sides[:, 0].reshape(1, 8, 128)])
    B = jnp.concatenate([B, sides[:, 1].reshape(1, 8, 128)])
    C, rC, D, rD = exchanged(A, B)
    sums = jnp.concatenate([C + rC, D + rD], axis=1)
    whole = jnp.concatenate([x, v, ax + sums[:3], av, sums[3:4]])
    mine = lax.dynamic_slice_in_dim(whole, (y_role * 2 + z_role) * 4, 4, axis=1)
    mine = jnp.swapaxes(mine, 0, 1)
    turned = lax.dynamic_slice_in_dim(jnp.concatenate([mine, mine]), (y_in_four + 1) % 4, 4)
    got = [send(turned[3 - t], [(q, p) for p, q in spread_pairs(t)]) for t in range(4)]
    stacked = jnp.stack(got)
    out = lax.dynamic_slice_in_dim(jnp.concatenate([stacked, stacked]), (4 - a) % 4, 4)
    out = out[None, :, None]
    return (
        out[:, :, :, 0:3],
        out[:, :, :, 3:6],
        out[:, :, :, 6:9],
        out[:, :, :, 9:12],
        out[:, :, :, 12] * alive[None, :, None],
    )


def solution(mesh):
    vector = P("gx", "gy", "gz", None, None)
    scalar = P("gx", "gy", "gz", None)
    block = P("gx", "gy", "gz")
    in_specs = (
        vector, vector, scalar, scalar, block, P(), P(), scalar, vector, block, vector, vector,
    )
    out_specs = (vector, vector, vector, vector, scalar)
    return jax.shard_map(on_device, mesh=mesh, in_specs=in_specs, out_specs=out_specs, check_vma=False)
```

```python
import functools

import jax
import jax.numpy as jnp
from jax import lax
from jax.experimental import pallas as pl
from jax.experimental.pallas import tpu as pltpu
from jax.sharding import PartitionSpec as P

STEPS = 5
SOFT = 0.04
KAPPA = 2.0
LOG2E = 1.4426950408889634
COULOMB = 4.0
TIME_STEP = 0.004
HALF = 0.5 * TIME_STEP
AXES = ("gx", "gy", "gz")
GRID = 16
OWN = 8
BLOCKS = 16
ROWS = 18
TILES = 4
GROUP = 8 * TILES
JOBS = 3
LIST = 56 * (128 // GROUP) + 16


def column_device(y, z):
    phys_y = y // 4
    phys_x = y % 4 if phys_y % 2 == 0 else 3 - y % 4
    phys_z = z // 2
    core = z % 2 if phys_z % 2 == 0 else 1 - z % 2
    return (phys_y * 4 + (phys_z % 2) * 2 + core) * 16 + (phys_z // 2) * 4 + phys_x


def column_of_device():
    gx, gy, gz = (lax.axis_index(name) for name in AXES)
    low, core = gy // 2, gy % 2
    high, phys_x = gz // 4, gz % 4
    phys_z = high * 2 + low
    y = gx * 4 + jnp.where(gx % 2 == 0, phys_x, 3 - phys_x)
    z = phys_z * 2 + jnp.where(phys_z % 2 == 0, core, 1 - core)
    return y, z


def spread_pairs(turn):
    return [
        ((a * 4 + b) * 16 + c, column_device(4 * b + (a + turn) % 4, c))
        for a in range(4)
        for b in range(4)
        for c in range(16)
    ]


def swap_pairs(axis, parity):
    pairs = []
    for y in range(GRID):
        for z in range(GRID):
            own = (y, z)[axis]
            other = own + 1 if own % 2 == parity else own - 1
            if 0 <= other < GRID:
                target = (other, z) if axis == 0 else (y, other)
                pairs.append((column_device(y, z), column_device(*target)))
    return pairs


def down_pairs(axis):
    pairs = []
    for y in range(GRID):
        for z in range(GRID):
            target = (y - 1, z) if axis == 0 else (y, z - 1)
            if min(target) >= 0:
                pairs.append((column_device(y, z), column_device(*target)))
    return pairs


def send(value, pairs):
    return lax.ppermute(value, AXES, pairs)


def list_kernel(list_ref, count_ref, place_ref, out_ref, total_ref):
    y_in_four, y_role, z_role = place_ref[0], place_ref[1], place_ref[2]
    total = jnp.int32(0)
    for a in range(4):

        count = jnp.minimum(list_ref[a, 112], 56)

        def one(k, total, a=a, count=count):
            def block(index):
                i = (index * 205) >> 11
                j = (index - 10 * i) >> 1
                return a + i, j, index & 1

            def number(x, j, l):
                return (((((j - y_in_four) & 1) ^ y_role) * 2 + (l ^ z_role)) * 4) + jnp.minimum(x, 3)

            first = block(list_ref[a, k])
            second = block(list_ref[a, 56 + k])
            mine = (jnp.minimum(first[1], second[1]) == y_in_four) & (k < count)
            one_number, two_number = number(*first), number(*second)
            one_count, two_count = count_ref[one_number], count_ref[two_number]
            swap = (first[2] > second[2]) | ((first[2] == second[2]) & (one_count > two_count))
            sign = jnp.where(swap, -1, 1)
            left = jnp.where(swap, two_number, one_number)
            right = jnp.where(swap, one_number, two_number)
            steps = (jnp.where(swap, two_count, one_count) + (GROUP - 1)) // GROUP
            own_left = ((left >> 3) << 2) + (left & 3)
            word = own_left + right * 16 + (jnp.where(left == right, 1, 2) << 18)
            for place in range(3):
                word = word + ((sign * (first[place] - second[place]) + 1) << (12 + 2 * place))
            for step in range(128 // GROUP):
                out_ref[total + step] = word + step * 256
            return total + jnp.where(mine, steps, 0)

        def four(k, total, one=one):
            for part in range(4):
                total = one(4 * k + part, total)
            return total

        total = lax.fori_loop(0, (count + 3) // 4, four, total)
    for job in range(JOBS):
        out_ref[total + job] = 0
    total_ref[0] = (total + JOBS - 1) // JOBS
    total_ref[1] = z_role


def inverse_of(value):
    guess = pl.reciprocal(value, approx=True)
    return guess * (2.0 - value * guess)


def sweep_tiles(mode, list_ref, total_ref, rows_ref, columns_refs, row_sum_ref, column_sum_ref):
    forces, pulled = "F" in mode, "J" in mode
    made = 3 * forces + 4 * pulled

    def one_job(word):
        left, right, step = word & 15, (word >> 4) & 15, (word >> 8) & 15
        offset = [(((word >> (12 + 2 * c)) & 3) - 1).astype(jnp.float32) for c in range(3)]
        weight = (word >> 18).astype(jnp.float32) * 0.5

        def row(c, scale=None, shift=None):
            value = rows_ref[c, pl.ds(right, 1), :]
            if scale is not None:
                value = value * scale
            if shift is not None:
                value = value - shift
            return jnp.broadcast_to(value, (8, 128))

        right_pos = [row(c, shift=offset[c]) for c in range(3)]
        right_charge = row(3, scale=8.0 * weight)
        right_half = row(4)
        right_depth = row(5, scale=24.0 * weight)
        right_cot = [row(6 + c) for c in range(3)] if pulled else None

        sums = None
        for tile in range(TILES):
            eight = pl.ds(pl.multiple_of(left * 128 + step * GROUP + 8 * tile, 8), 8)

            def column(c):
                return columns_refs[c // 3][c % 3, eight, :]

            d = [column(c) - right_pos[c] for c in range(3)]
            charge = column(3)
            half = column(4) + right_half
            depth = column(5) * right_depth
            s = d[0] * d[0] + d[1] * d[1] + d[2] * d[2]
            sigma2 = half * half
            r = inverse_of(s + sigma2)
            t = sigma2 * r
            p = t * t * t
            soft = s + SOFT
            ir = lax.rsqrt(soft)
            g = jnp.exp2((soft * ir) * (-KAPPA * LOG2E)) * ir
            fade = jnp.maximum(1.0 - s, 0.0)
            fade2 = fade * fade
            fr = fade * r
            ir2 = ir * ir
            fade_kappa = fade * (ir + 0.5 * ir2)
            fade2h = fade2 * (g * (3.0 + fade_kappa))
            dp = depth * p
            charges = charge * right_charge
            A = (fade2 * dp) * ((p - 1.0) + fr * (2.0 * p - 1.0)) + charges * fade2h
            values = []
            if forces:
                values += [A * d[c] for c in range(3)]
            if pulled:
                w = [column(6 + c) - right_cot[c] for c in range(3)]
                dw = d[0] * w[0] + d[1] * w[1] + d[2] * w[2]
                lj = (2.0 * p - 2.0) + fr * ((12.0 * p - 6.0) + fr * (14.0 * p - 4.0))
                m2 = ir2 * (1.0 + 1.5 * ir + 0.75 * ir2)
                coulomb = 6.0 * (1.0 + fade_kappa) + fade2 * m2
                B = (-2.0 * fade) * (dp * lj + (charges * g) * coulomb) * dw
                values += [A * w[c] + B * d[c] for c in range(3)]
                common = fade2h * dw
                values += [common * right_charge]
                last = common * charge
            for place, value in enumerate(values):
                row_sum_ref[place, eight, :] = row_sum_ref[place, eight, :] + value
            if pulled:
                values[-1] = -last
            sums = values if sums is None else [a + b for a, b in zip(sums, values)]
        if pulled:
            sums[-1] = sums[-1] * (8.0 * weight)
        for place in range(made):
            column_sum_ref[place, right] = column_sum_ref[place, right] + sums[place]

    def one_step(k, carry):
        for job in range(JOBS):
            one_job(list_ref[k * JOBS + job])
        return carry

    lax.fori_loop(0, total_ref[0], one_step, jnp.int32(0))


def sweep_kernel(mode, first, kick, list_ref, total_ref, *refs):
    forces, pulled = "F" in mode, "J" in mode
    made = 3 * forces + 4 * pulled
    names = ["ext"] + (["params"] if not first or mode == "J" else []) + (["places"] if mode == "J" else [])
    if mode != "J":
        names += ["x", "v"] if not first else []
        names += [] if first else ["C", "rC", "D", "rD"]
    else:
        names += ["x", "ax", "av", "C", "rC", "D", "rD", "charge"] + (["v"] if first else [])
    outs = ["A", "B"] + (["places"] if mode != "J" else []) + (["params"] if mode == "F" and first else [])
    if mode == "F" and not first:
        outs += ["x_out", "v_out"]
    if mode == "FJ":
        outs += ["x_out", "v_out", "charge_out"]
    if mode == "J":
        outs += ["ax_out", "av_out", "charge_out"] + (["v_out"] if first else [])
    scratch = ["rows", "cotangents", "row_sum", "column_sum"]
    r = dict(zip(names + outs + scratch, refs))
    ext = r["ext"]
    inverse = ext[9]

    def received(c):
        return jnp.concatenate([r["C"][c] + r["rC"][c], r["D"][c] + r["rD"][c]], axis=0)

    position, cotangent = [], []
    for c in range(3):
        if mode != "J":
            if first:
                position.append(ext[c])
            else:
                velocity = r["v"][c] + kick * inverse * received(c)
                position.append(r["x"][c] + TIME_STEP * velocity)
                r["x_out"][c] = position[c]
                r["v_out"][c] = velocity
            if pulled:
                cotangent.append(HALF * inverse * ext[13 + c])
        else:
            if first:
                r["v_out"][c] = r["v"][c] + HALF * inverse * received(c)
            ax = r["ax"][c] + received(c + 3 if first else c)
            av = r["av"][c] + TIME_STEP * ax
            r["ax_out"][c] = ax
            r["av_out"][c] = av
            position.append(r["x"][c])
            cotangent.append(kick * inverse * av)
    _spread_and_sweep(mode, first, ext, position, cotangent, list_ref, total_ref, r, made, pulled)


def _spread_and_sweep(mode, first, ext, position, cotangent, list_ref, total_ref, r, made, pulled):
    rows = r["rows"]
    own_first = total_ref[1] == 0
    quantities = position + [ext[6], 0.5 * ext[7], ext[8]] + cotangent
    for place, value in enumerate(quantities):
        rows[place] = value
        fresh = (mode != "J", mode == "F" and first, True)[place // 3]
        if not fresh:
            continue
        target = (r["places"], r.get("params"), r["cotangents"])[place // 3]
        near = jnp.concatenate([value[0:4], value[8:12]], axis=0)
        far = jnp.concatenate([value[4:8], value[12:16]], axis=0)
        turned = jnp.where(own_first, near, far).T
        for e in range(OWN):
            target[place % 3, e * 128 : (e + 1) * 128, :] = jnp.broadcast_to(turned[:, e : e + 1], (128, 128))
    r["row_sum"][...] = jnp.zeros(r["row_sum"].shape, jnp.float32)
    r["column_sum"][...] = jnp.zeros(r["column_sum"].shape, jnp.float32)
    sweep_tiles(mode, list_ref, total_ref, rows, (r["places"], r["params"], r["cotangents"]), r["row_sum"], r["column_sum"])
    lane = lax.broadcasted_iota(jnp.int32, (128, OWN), 1)
    for c in range(made):
        by_atom = jnp.zeros((128, OWN), jnp.float32)
        for e in range(OWN):
            total = jnp.sum(r["row_sum"][c, e * 128 : (e + 1) * 128, :], axis=1, keepdims=True)
            by_atom = jnp.where(lane == e, jnp.broadcast_to(total, (128, OWN)), by_atom)
        own = by_atom.T
        others = jnp.sum(r["column_sum"][c], axis=1)
        A = jnp.where(own_first, own, 0.0) - jnp.concatenate([others[0:4], others[8:12]], axis=0)
        B = jnp.where(own_first, 0.0, own) - jnp.concatenate([others[4:8], others[12:16]], axis=0)
        if pulled and c == made - 1:
            total = jnp.concatenate([A[0:4], B[0:4], A[4:8], B[4:8]], axis=0)
            if mode == "J":
                total = total + r["charge"][...]
            r["charge_out"][...] = total
        else:
            r["A"][c] = A
            r["B"][c] = B


def sweep(mode, first, kick, plist, total, arrays):
    forces, pulled = "F" in mode, "J" in mode
    sent = 3 * forces + 3 * pulled
    made = 3 * forces + 4 * pulled
    quantities = 6 + 3 * pulled
    f32 = jnp.float32
    exchange = jax.ShapeDtypeStruct((sent, 8, 128), f32)
    vector = jax.ShapeDtypeStruct((3, BLOCKS, 128), f32)
    scalar = jax.ShapeDtypeStruct((BLOCKS, 128), f32)
    wide = jax.ShapeDtypeStruct((3, OWN * 128, 128), f32)
    outs = [exchange, exchange] + ([wide] if mode != "J" else []) + ([wide] if mode == "F" and first else [])
    if mode == "F" and not first:
        outs += [vector, vector]
    if mode == "FJ":
        outs += [vector, vector, scalar]
    if mode == "J":
        outs += [vector, vector, scalar] + ([vector] if first else [])
    vmem = pl.BlockSpec(memory_space=pltpu.VMEM)
    smem = pl.BlockSpec(memory_space=pltpu.SMEM)
    return pl.pallas_call(
        functools.partial(sweep_kernel, mode, first, kick),
        out_shape=outs,
        in_specs=[smem, smem] + [vmem] * len(arrays),
        out_specs=[vmem] * len(outs),
        scratch_shapes=[
            pltpu.VMEM((quantities, BLOCKS, 128), f32),
            pltpu.VMEM((3, OWN * 128 if pulled else 8, 128), f32),
            pltpu.VMEM((made, OWN * 128, 128), f32),
            pltpu.VMEM((made, BLOCKS, 8, 128), f32),
        ],
        compiler_params=pltpu.CompilerParams(vmem_limit_bytes=32 * 1024 * 1024),
        name=f"sweep_{mode}",
    )(plist, total, *arrays)


def exchanged(A, B):
    rA, rB = send(A, swap_pairs(1, 0)), send(B, swap_pairs(1, 1))
    T0, T1 = A + rA, B + rB
    C = jnp.concatenate([T0[:, 0:4], T1[:, 0:4]], axis=1)
    D = jnp.concatenate([T0[:, 4:8], T1[:, 4:8]], axis=1)
    return C, send(C, swap_pairs(0, 0)), D, send(D, swap_pairs(0, 1))


def on_device(
    positions,
    velocities,
    charges,
    atom_types,
    atom_count,
    sigma_type,
    epsilon_type,
    masses,
    pair_list,
    pair_count,
    pos_cotangent,
    vel_cotangent,
):
    f32 = jnp.float32
    a = lax.axis_index("gx")
    y, z = column_of_device()
    y_even, z_even = y % 2 == 0, z % 2 == 0
    counts = atom_count[0, :, 0]
    alive = (lax.broadcasted_iota(jnp.int32, (4, 128), 1) < counts[:, None]).astype(f32)
    kinds = (atom_types[0, :, 0][:, None, :] == lax.broadcasted_iota(jnp.int32, (16, 1), 0)).astype(f32)
    sigma = jnp.sum(kinds * sigma_type[:, None], axis=1)
    epsilon = jnp.sum(kinds * epsilon_type[:, None], axis=1)
    listed = jnp.concatenate(
        [pair_list[0, 0, 0].reshape(112), jnp.broadcast_to(pair_count[0, 0, 0], (16,))]
    ).astype(f32)
    bundle = jnp.concatenate(
        [
            positions[0, :, 0],
            velocities[0, :, 0],
            jnp.stack(
                [charges[0, :, 0] * alive, sigma, jnp.sqrt(epsilon) * alive, 1.0 / masses[0, :, 0]], axis=1
            ),
            pos_cotangent[0, :, 0],
            vel_cotangent[0, :, 0],
            jnp.broadcast_to(counts.astype(f32)[:, None, None], (4, 1, 128)),
            jnp.broadcast_to(listed[None, None, :], (4, 1, 128)),
        ],
        axis=1,
    )
    turned = lax.dynamic_slice_in_dim(jnp.concatenate([bundle, bundle]), a, 4)
    got = [send(turned[t], spread_pairs(t)) for t in range(4)]
    stacked = jnp.stack(got[::-1])
    y_in_four = y % 4
    own = lax.dynamic_slice_in_dim(jnp.concatenate([stacked, stacked]), 3 - y_in_four, 4)
    own = jnp.swapaxes(own, 0, 1)
    lists = own[17].astype(jnp.int32)
    own = own[:17]
    upper = send(own, down_pairs(1))
    wide = jnp.where(
        z_even, jnp.concatenate([upper, own], axis=1), jnp.concatenate([own, upper], axis=1)
    )
    upper = send(wide, down_pairs(0))
    ext = jnp.where(
        y_even, jnp.concatenate([upper, wide], axis=1), jnp.concatenate([wide, upper], axis=1)
    )
    y_role, z_role = jnp.where(y_even, 1, 0), jnp.where(z_even, 1, 0)
    smem = pl.BlockSpec(memory_space=pltpu.SMEM)
    plist, total = pl.pallas_call(
        list_kernel,
        out_shape=[jax.ShapeDtypeStruct((LIST,), jnp.int32), jax.ShapeDtypeStruct((2,), jnp.int32)],
        in_specs=[smem] * 3,
        out_specs=[smem] * 2,
        name="keep_pairs",
    )(
        lists,
        ext[16, :, 0].astype(jnp.int32),
        jnp.stack([y_in_four, y_role, z_role]).astype(jnp.int32),
    )
    A, B, places, params = sweep("F", True, 0.0, plist, total, [ext])
    history = [(ext[0:3], places)]
    x, v = ext[0:3], ext[3:6]
    for step in range(STEPS):
        parts = exchanged(A, B)
        kick = HALF if step == 0 else TIME_STEP
        mode = "F" if step < STEPS - 1 else "FJ"
        A, B, places, x, v, *rest = sweep(mode, False, kick, plist, total, [ext, params, x, v, *parts])
        history.append((x, places))
    charge = rest[0]
    ax, av = ext[10:13], ext[13:16]
    for step in range(STEPS - 1, -1, -1):
        parts = exchanged(A, B)
        first = step == STEPS - 1
        factor = TIME_STEP if step > 0 else HALF
        A, B, ax, av, charge, *rest = sweep(
            "J",
            first,
            factor,
            plist,
            total,
            [ext, params, history[step][1], history[step][0], ax, av, *parts, charge] + ([v] if first else []),
        )
        if first:
            v = rest[0]
    sides = charge.reshape(2, 2, 4, 128)
    A = jnp.concatenate([A, sides[:, 0].reshape(1, 8, 128)])
    B = jnp.concatenate([B, sides[:, 1].reshape(1, 8, 128)])
    C, rC, D, rD = exchanged(A, B)
    sums = jnp.concatenate([C + rC, D + rD], axis=1)
    whole = jnp.concatenate([x, v, ax + sums[:3], av, sums[3:4]])
    mine = lax.dynamic_slice_in_dim(whole, (y_role * 2 + z_role) * 4, 4, axis=1)
    mine = jnp.swapaxes(mine, 0, 1)
    turned = lax.dynamic_slice_in_dim(jnp.concatenate([mine, mine]), (y_in_four + 1) % 4, 4)
    got = [send(turned[3 - t], [(q, p) for p, q in spread_pairs(t)]) for t in range(4)]
    stacked = jnp.stack(got)
    out = lax.dynamic_slice_in_dim(jnp.concatenate([stacked, stacked]), (4 - a) % 4, 4)
    out = out[None, :, None]
    return (
        out[:, :, :, 0:3],
        out[:, :, :, 3:6],
        out[:, :, :, 6:9],
        out[:, :, :, 9:12],
        out[:, :, :, 12] * alive[None, :, None],
    )


def solution(mesh):
    vector = P("gx", "gy", "gz", None, None)
    scalar = P("gx", "gy", "gz", None)
    block = P("gx", "gy", "gz")
    in_specs = (
        vector, vector, scalar, scalar, block, P(), P(), scalar, vector, block, vector, vector,
    )
    out_specs = (vector, vector, vector, vector, scalar)
    return jax.shard_map(on_device, mesh=mesh, in_specs=in_specs, out_specs=out_specs, check_vma=False)
```

```python
import functools

import jax
import jax.numpy as jnp
from jax import lax
from jax.experimental import pallas as pl
from jax.experimental.pallas import tpu as pltpu
from jax.sharding import PartitionSpec as P

STEPS = 5
SOFT = 0.04
KAPPA = 2.0
LOG2E = 1.4426950408889634
COULOMB = 4.0
TIME_STEP = 0.004
HALF = 0.5 * TIME_STEP
AXES = ("gx", "gy", "gz")
GRID = 16
OWN = 8
BLOCKS = 16
ROWS = 18
TILES = 2
GROUP = 8 * TILES
JOBS = 6
LIST = 56 * (128 // GROUP) + 16


def column_device(y, z):
    phys_y = y // 4
    phys_x = y % 4 if phys_y % 2 == 0 else 3 - y % 4
    phys_z = z // 2
    core = z % 2 if phys_z % 2 == 0 else 1 - z % 2
    return (phys_y * 4 + (phys_z % 2) * 2 + core) * 16 + (phys_z // 2) * 4 + phys_x


def column_of_device():
    gx, gy, gz = (lax.axis_index(name) for name in AXES)
    low, core = gy // 2, gy % 2
    high, phys_x = gz // 4, gz % 4
    phys_z = high * 2 + low
    y = gx * 4 + jnp.where(gx % 2 == 0, phys_x, 3 - phys_x)
    z = phys_z * 2 + jnp.where(phys_z % 2 == 0, core, 1 - core)
    return y, z


def spread_pairs(turn):
    return [
        ((a * 4 + b) * 16 + c, column_device(4 * b + (a + turn) % 4, c))
        for a in range(4)
        for b in range(4)
        for c in range(16)
    ]


def swap_pairs(axis, parity):
    pairs = []
    for y in range(GRID):
        for z in range(GRID):
            own = (y, z)[axis]
            other = own + 1 if own % 2 == parity else own - 1
            if 0 <= other < GRID:
                target = (other, z) if axis == 0 else (y, other)
                pairs.append((column_device(y, z), column_device(*target)))
    return pairs


def down_pairs(axis):
    pairs = []
    for y in range(GRID):
        for z in range(GRID):
            target = (y - 1, z) if axis == 0 else (y, z - 1)
            if min(target) >= 0:
                pairs.append((column_device(y, z), column_device(*target)))
    return pairs


def send(value, pairs):
    return lax.ppermute(value, AXES, pairs)


def list_kernel(list_ref, count_ref, place_ref, out_ref, total_ref):
    y_in_four, y_role, z_role = place_ref[0], place_ref[1], place_ref[2]
    total = jnp.int32(0)
    for a in range(4):

        count = jnp.minimum(list_ref[a, 112], 56)

        def one(k, total, a=a, count=count):
            def block(index):
                i = (index * 205) >> 11
                j = (index - 10 * i) >> 1
                return a + i, j, index & 1

            def number(x, j, l):
                return (((((j - y_in_four) & 1) ^ y_role) * 2 + (l ^ z_role)) * 4) + jnp.minimum(x, 3)

            first = block(list_ref[a, k])
            second = block(list_ref[a, 56 + k])
            mine = (jnp.minimum(first[1], second[1]) == y_in_four) & (k < count)
            one_number, two_number = number(*first), number(*second)
            one_count, two_count = count_ref[one_number], count_ref[two_number]
            swap = (first[2] > second[2]) | ((first[2] == second[2]) & (one_count > two_count))
            sign = jnp.where(swap, -1, 1)
            left = jnp.where(swap, two_number, one_number)
            right = jnp.where(swap, one_number, two_number)
            steps = (jnp.where(swap, two_count, one_count) + (GROUP - 1)) // GROUP
            own_left = ((left >> 3) << 2) + (left & 3)
            word = own_left + right * 16 + (jnp.where(left == right, 1, 2) << 18)
            for place in range(3):
                word = word + ((sign * (first[place] - second[place]) + 1) << (12 + 2 * place))
            for step in range(128 // GROUP):
                out_ref[total + step] = word + step * 256
            return total + jnp.where(mine, steps, 0)

        def four(k, total, one=one):
            for part in range(4):
                total = one(4 * k + part, total)
            return total

        total = lax.fori_loop(0, (count + 3) // 4, four, total)
    for job in range(JOBS):
        out_ref[total + job] = 0
    total_ref[0] = (total + JOBS - 1) // JOBS
    total_ref[1] = z_role


def inverse_of(value):
    guess = pl.reciprocal(value, approx=True)
    return guess * (2.0 - value * guess)


def sweep_tiles(mode, list_ref, total_ref, rows_ref, columns_refs, row_sum_ref, column_sum_ref):
    forces, pulled = "F" in mode, "J" in mode
    made = 3 * forces + 4 * pulled

    def one_job(word):
        left, right, step = word & 15, (word >> 4) & 15, (word >> 8) & 15
        offset = [(((word >> (12 + 2 * c)) & 3) - 1).astype(jnp.float32) for c in range(3)]
        weight = (word >> 18).astype(jnp.float32) * 0.5

        def row(c, scale=None, shift=None):
            value = rows_ref[c, pl.ds(right, 1), :]
            if scale is not None:
                value = value * scale
            if shift is not None:
                value = value - shift
            return jnp.broadcast_to(value, (8, 128))

        right_pos = [row(c, shift=offset[c]) for c in range(3)]
        right_charge = row(3, scale=8.0 * weight)
        right_half = row(4)
        right_depth = row(5, scale=24.0 * weight)
        right_cot = [row(6 + c) for c in range(3)] if pulled else None

        sums = None
        for tile in range(TILES):
            eight = pl.ds(pl.multiple_of(left * 128 + step * GROUP + 8 * tile, 8), 8)

            def column(c):
                return columns_refs[c // 3][c % 3, eight, :]

            d = [column(c) - right_pos[c] for c in range(3)]
            charge = column(3)
            half = column(4) + right_half
            depth = column(5) * right_depth
            s = d[0] * d[0] + d[1] * d[1] + d[2] * d[2]
            sigma2 = half * half
            r = inverse_of(s + sigma2)
            t = sigma2 * r
            p = t * t * t
            soft = s + SOFT
            ir = lax.rsqrt(soft)
            g = jnp.exp2((soft * ir) * (-KAPPA * LOG2E)) * ir
            fade = jnp.maximum(1.0 - s, 0.0)
            fade2 = fade * fade
            fr = fade * r
            ir2 = ir * ir
            fade_kappa = fade * (ir + 0.5 * ir2)
            fade2h = fade2 * (g * (3.0 + fade_kappa))
            dp = depth * p
            charges = charge * right_charge
            A = (fade2 * dp) * ((p - 1.0) + fr * (2.0 * p - 1.0)) + charges * fade2h
            values = []
            if forces:
                values += [A * d[c] for c in range(3)]
            if pulled:
                w = [column(6 + c) - right_cot[c] for c in range(3)]
                dw = d[0] * w[0] + d[1] * w[1] + d[2] * w[2]
                lj = (2.0 * p - 2.0) + fr * ((12.0 * p - 6.0) + fr * (14.0 * p - 4.0))
                m2 = ir2 * (1.0 + 1.5 * ir + 0.75 * ir2)
                coulomb = 6.0 * (1.0 + fade_kappa) + fade2 * m2
                B = (-2.0 * fade) * (dp * lj + (charges * g) * coulomb) * dw
                values += [A * w[c] + B * d[c] for c in range(3)]
                common = fade2h * dw
                values += [common * right_charge]
                last = common * charge
            for place, value in enumerate(values):
                row_sum_ref[place, eight, :] = row_sum_ref[place, eight, :] + value
            if pulled:
                values[-1] = -last
            sums = values if sums is None else [a + b for a, b in zip(sums, values)]
        if pulled:
            sums[-1] = sums[-1] * (8.0 * weight)
        for place in range(made):
            column_sum_ref[place, right] = column_sum_ref[place, right] + sums[place]

    def one_step(k, carry):
        for job in range(JOBS):
            one_job(list_ref[k * JOBS + job])
        return carry

    lax.fori_loop(0, total_ref[0], one_step, jnp.int32(0))


def sweep_kernel(mode, first, kick, list_ref, total_ref, *refs):
    forces, pulled = "F" in mode, "J" in mode
    made = 3 * forces + 4 * pulled
    names = ["ext"] + (["params"] if not first or mode == "J" else []) + (["places"] if mode == "J" else [])
    if mode != "J":
        names += ["x", "v"] if not first else []
        names += [] if first else ["C", "rC", "D", "rD"]
    else:
        names += ["x", "ax", "av", "C", "rC", "D", "rD", "charge"] + (["v"] if first else [])
    outs = ["A", "B"] + (["places"] if mode != "J" else []) + (["params"] if mode == "F" and first else [])
    if mode == "F" and not first:
        outs += ["x_out", "v_out"]
    if mode == "FJ":
        outs += ["x_out", "v_out", "charge_out"]
    if mode == "J":
        outs += ["ax_out", "av_out", "charge_out"] + (["v_out"] if first else [])
    scratch = ["rows", "cotangents", "row_sum", "column_sum"]
    r = dict(zip(names + outs + scratch, refs))
    ext = r["ext"]
    inverse = ext[9]

    def received(c):
        return jnp.concatenate([r["C"][c] + r["rC"][c], r["D"][c] + r["rD"][c]], axis=0)

    position, cotangent = [], []
    for c in range(3):
        if mode != "J":
            if first:
                position.append(ext[c])
            else:
                velocity = r["v"][c] + kick * inverse * received(c)
                position.append(r["x"][c] + TIME_STEP * velocity)
                r["x_out"][c] = position[c]
                r["v_out"][c] = velocity
            if pulled:
                cotangent.append(HALF * inverse * ext[13 + c])
        else:
            if first:
                r["v_out"][c] = r["v"][c] + HALF * inverse * received(c)
            ax = r["ax"][c] + received(c + 3 if first else c)
            av = r["av"][c] + TIME_STEP * ax
            r["ax_out"][c] = ax
            r["av_out"][c] = av
            position.append(r["x"][c])
            cotangent.append(kick * inverse * av)
    _spread_and_sweep(mode, first, ext, position, cotangent, list_ref, total_ref, r, made, pulled)


def _spread_and_sweep(mode, first, ext, position, cotangent, list_ref, total_ref, r, made, pulled):
    rows = r["rows"]
    own_first = total_ref[1] == 0
    quantities = position + [ext[6], 0.5 * ext[7], ext[8]] + cotangent
    for place, value in enumerate(quantities):
        rows[place] = value
        fresh = (mode != "J", mode == "F" and first, True)[place // 3]
        if not fresh:
            continue
        target = (r["places"], r.get("params"), r["cotangents"])[place // 3]
        near = jnp.concatenate([value[0:4], value[8:12]], axis=0)
        far = jnp.concatenate([value[4:8], value[12:16]], axis=0)
        turned = jnp.where(own_first, near, far).T
        for e in range(OWN):
            target[place % 3, e * 128 : (e + 1) * 128, :] = jnp.broadcast_to(turned[:, e : e + 1], (128, 128))
    r["row_sum"][...] = jnp.zeros(r["row_sum"].shape, jnp.float32)
    r["column_sum"][...] = jnp.zeros(r["column_sum"].shape, jnp.float32)
    sweep_tiles(mode, list_ref, total_ref, rows, (r["places"], r["params"], r["cotangents"]), r["row_sum"], r["column_sum"])
    lane = lax.broadcasted_iota(jnp.int32, (128, OWN), 1)
    for c in range(made):
        by_atom = jnp.zeros((128, OWN), jnp.float32)
        for e in range(OWN):
            total = jnp.sum(r["row_sum"][c, e * 128 : (e + 1) * 128, :], axis=1, keepdims=True)
            by_atom = jnp.where(lane == e, jnp.broadcast_to(total, (128, OWN)), by_atom)
        own = by_atom.T
        others = jnp.sum(r["column_sum"][c], axis=1)
        A = jnp.where(own_first, own, 0.0) - jnp.concatenate([others[0:4], others[8:12]], axis=0)
        B = jnp.where(own_first, 0.0, own) - jnp.concatenate([others[4:8], others[12:16]], axis=0)
        if pulled and c == made - 1:
            total = jnp.concatenate([A[0:4], B[0:4], A[4:8], B[4:8]], axis=0)
            if mode == "J":
                total = total + r["charge"][...]
            r["charge_out"][...] = total
        else:
            r["A"][c] = A
            r["B"][c] = B


def sweep(mode, first, kick, plist, total, arrays):
    forces, pulled = "F" in mode, "J" in mode
    sent = 3 * forces + 3 * pulled
    made = 3 * forces + 4 * pulled
    quantities = 6 + 3 * pulled
    f32 = jnp.float32
    exchange = jax.ShapeDtypeStruct((sent, 8, 128), f32)
    vector = jax.ShapeDtypeStruct((3, BLOCKS, 128), f32)
    scalar = jax.ShapeDtypeStruct((BLOCKS, 128), f32)
    wide = jax.ShapeDtypeStruct((3, OWN * 128, 128), f32)
    outs = [exchange, exchange] + ([wide] if mode != "J" else []) + ([wide] if mode == "F" and first else [])
    if mode == "F" and not first:
        outs += [vector, vector]
    if mode == "FJ":
        outs += [vector, vector, scalar]
    if mode == "J":
        outs += [vector, vector, scalar] + ([vector] if first else [])
    vmem = pl.BlockSpec(memory_space=pltpu.VMEM)
    smem = pl.BlockSpec(memory_space=pltpu.SMEM)
    return pl.pallas_call(
        functools.partial(sweep_kernel, mode, first, kick),
        out_shape=outs,
        in_specs=[smem, smem] + [vmem] * len(arrays),
        out_specs=[vmem] * len(outs),
        scratch_shapes=[
            pltpu.VMEM((quantities, BLOCKS, 128), f32),
            pltpu.VMEM((3, OWN * 128 if pulled else 8, 128), f32),
            pltpu.VMEM((made, OWN * 128, 128), f32),
            pltpu.VMEM((made, BLOCKS, 8, 128), f32),
        ],
        compiler_params=pltpu.CompilerParams(vmem_limit_bytes=32 * 1024 * 1024),
        name=f"sweep_{mode}",
    )(plist, total, *arrays)


def exchanged(A, B):
    rA, rB = send(A, swap_pairs(1, 0)), send(B, swap_pairs(1, 1))
    T0, T1 = A + rA, B + rB
    C = jnp.concatenate([T0[:, 0:4], T1[:, 0:4]], axis=1)
    D = jnp.concatenate([T0[:, 4:8], T1[:, 4:8]], axis=1)
    return C, send(C, swap_pairs(0, 0)), D, send(D, swap_pairs(0, 1))


def on_device(
    positions,
    velocities,
    charges,
    atom_types,
    atom_count,
    sigma_type,
    epsilon_type,
    masses,
    pair_list,
    pair_count,
    pos_cotangent,
    vel_cotangent,
):
    f32 = jnp.float32
    a = lax.axis_index("gx")
    y, z = column_of_device()
    y_even, z_even = y % 2 == 0, z % 2 == 0
    counts = atom_count[0, :, 0]
    alive = (lax.broadcasted_iota(jnp.int32, (4, 128), 1) < counts[:, None]).astype(f32)
    kinds = (atom_types[0, :, 0][:, None, :] == lax.broadcasted_iota(jnp.int32, (16, 1), 0)).astype(f32)
    sigma = jnp.sum(kinds * sigma_type[:, None], axis=1)
    epsilon = jnp.sum(kinds * epsilon_type[:, None], axis=1)
    listed = jnp.concatenate(
        [pair_list[0, 0, 0].reshape(112), jnp.broadcast_to(pair_count[0, 0, 0], (16,))]
    ).astype(f32)
    bundle = jnp.concatenate(
        [
            positions[0, :, 0],
            velocities[0, :, 0],
            jnp.stack(
                [charges[0, :, 0] * alive, sigma, jnp.sqrt(epsilon) * alive, 1.0 / masses[0, :, 0]], axis=1
            ),
            pos_cotangent[0, :, 0],
            vel_cotangent[0, :, 0],
            jnp.broadcast_to(counts.astype(f32)[:, None, None], (4, 1, 128)),
            jnp.broadcast_to(listed[None, None, :], (4, 1, 128)),
        ],
        axis=1,
    )
    turned = lax.dynamic_slice_in_dim(jnp.concatenate([bundle, bundle]), a, 4)
    got = [send(turned[t], spread_pairs(t)) for t in range(4)]
    stacked = jnp.stack(got[::-1])
    y_in_four = y % 4
    own = lax.dynamic_slice_in_dim(jnp.concatenate([stacked, stacked]), 3 - y_in_four, 4)
    own = jnp.swapaxes(own, 0, 1)
    lists = own[17].astype(jnp.int32)
    own = own[:17]
    upper = send(own, down_pairs(1))
    wide = jnp.where(
        z_even, jnp.concatenate([upper, own], axis=1), jnp.concatenate([own, upper], axis=1)
    )
    upper = send(wide, down_pairs(0))
    ext = jnp.where(
        y_even, jnp.concatenate([upper, wide], axis=1), jnp.concatenate([wide, upper], axis=1)
    )
    y_role, z_role = jnp.where(y_even, 1, 0), jnp.where(z_even, 1, 0)
    smem = pl.BlockSpec(memory_space=pltpu.SMEM)
    plist, total = pl.pallas_call(
        list_kernel,
        out_shape=[jax.ShapeDtypeStruct((LIST,), jnp.int32), jax.ShapeDtypeStruct((2,), jnp.int32)],
        in_specs=[smem] * 3,
        out_specs=[smem] * 2,
        name="keep_pairs",
    )(
        lists,
        ext[16, :, 0].astype(jnp.int32),
        jnp.stack([y_in_four, y_role, z_role]).astype(jnp.int32),
    )
    A, B, places, params = sweep("F", True, 0.0, plist, total, [ext])
    history = [(ext[0:3], places)]
    x, v = ext[0:3], ext[3:6]
    for step in range(STEPS):
        parts = exchanged(A, B)
        kick = HALF if step == 0 else TIME_STEP
        mode = "F" if step < STEPS - 1 else "FJ"
        A, B, places, x, v, *rest = sweep(mode, False, kick, plist, total, [ext, params, x, v, *parts])
        history.append((x, places))
    charge = rest[0]
    ax, av = ext[10:13], ext[13:16]
    for step in range(STEPS - 1, -1, -1):
        parts = exchanged(A, B)
        first = step == STEPS - 1
        factor = TIME_STEP if step > 0 else HALF
        A, B, ax, av, charge, *rest = sweep(
            "J",
            first,
            factor,
            plist,
            total,
            [ext, params, history[step][1], history[step][0], ax, av, *parts, charge] + ([v] if first else []),
        )
        if first:
            v = rest[0]
    sides = charge.reshape(2, 2, 4, 128)
    A = jnp.concatenate([A, sides[:, 0].reshape(1, 8, 128)])
    B = jnp.concatenate([B, sides[:, 1].reshape(1, 8, 128)])
    C, rC, D, rD = exchanged(A, B)
    sums = jnp.concatenate([C + rC, D + rD], axis=1)
    whole = jnp.concatenate([x, v, ax + sums[:3], av, sums[3:4]])
    mine = lax.dynamic_slice_in_dim(whole, (y_role * 2 + z_role) * 4, 4, axis=1)
    mine = jnp.swapaxes(mine, 0, 1)
    turned = lax.dynamic_slice_in_dim(jnp.concatenate([mine, mine]), (y_in_four + 1) % 4, 4)
    got = [send(turned[3 - t], [(q, p) for p, q in spread_pairs(t)]) for t in range(4)]
    stacked = jnp.stack(got)
    out = lax.dynamic_slice_in_dim(jnp.concatenate([stacked, stacked]), (4 - a) % 4, 4)
    out = out[None, :, None]
    return (
        out[:, :, :, 0:3],
        out[:, :, :, 3:6],
        out[:, :, :, 6:9],
        out[:, :, :, 9:12],
        out[:, :, :, 12] * alive[None, :, None],
    )


def solution(mesh):
    vector = P("gx", "gy", "gz", None, None)
    scalar = P("gx", "gy", "gz", None)
    block = P("gx", "gy", "gz")
    in_specs = (
        vector, vector, scalar, scalar, block, P(), P(), scalar, vector, block, vector, vector,
    )
    out_specs = (vector, vector, vector, vector, scalar)
    return jax.shard_map(on_device, mesh=mesh, in_specs=in_specs, out_specs=out_specs, check_vma=False)
```

```python
import functools

import jax
import jax.numpy as jnp
from jax import lax
from jax.experimental import pallas as pl
from jax.experimental.pallas import tpu as pltpu
from jax.sharding import PartitionSpec as P

STEPS = 5
SOFT = 0.04
KAPPA = 2.0
LOG2E = 1.4426950408889634
COULOMB = 4.0
TIME_STEP = 0.004
HALF = 0.5 * TIME_STEP
AXES = ("gx", "gy", "gz")
GRID = 16
OWN = 8
BLOCKS = 16
ROWS = 18
TILES = 2
GROUP = 8 * TILES
JOBS = 8
LIST = 56 * (128 // GROUP) + 16


def column_device(y, z):
    phys_y = y // 4
    phys_x = y % 4 if phys_y % 2 == 0 else 3 - y % 4
    phys_z = z // 2
    core = z % 2 if phys_z % 2 == 0 else 1 - z % 2
    return (phys_y * 4 + (phys_z % 2) * 2 + core) * 16 + (phys_z // 2) * 4 + phys_x


def column_of_device():
    gx, gy, gz = (lax.axis_index(name) for name in AXES)
    low, core = gy // 2, gy % 2
    high, phys_x = gz // 4, gz % 4
    phys_z = high * 2 + low
    y = gx * 4 + jnp.where(gx % 2 == 0, phys_x, 3 - phys_x)
    z = phys_z * 2 + jnp.where(phys_z % 2 == 0, core, 1 - core)
    return y, z


def spread_pairs(turn):
    return [
        ((a * 4 + b) * 16 + c, column_device(4 * b + (a + turn) % 4, c))
        for a in range(4)
        for b in range(4)
        for c in range(16)
    ]


def swap_pairs(axis, parity):
    pairs = []
    for y in range(GRID):
        for z in range(GRID):
            own = (y, z)[axis]
            other = own + 1 if own % 2 == parity else own - 1
            if 0 <= other < GRID:
                target = (other, z) if axis == 0 else (y, other)
                pairs.append((column_device(y, z), column_device(*target)))
    return pairs


def down_pairs(axis):
    pairs = []
    for y in range(GRID):
        for z in range(GRID):
            target = (y - 1, z) if axis == 0 else (y, z - 1)
            if min(target) >= 0:
                pairs.append((column_device(y, z), column_device(*target)))
    return pairs


def send(value, pairs):
    return lax.ppermute(value, AXES, pairs)


def list_kernel(list_ref, count_ref, place_ref, out_ref, total_ref):
    y_in_four, y_role, z_role = place_ref[0], place_ref[1], place_ref[2]
    total = jnp.int32(0)
    for a in range(4):

        count = jnp.minimum(list_ref[a, 112], 56)

        def one(k, total, a=a, count=count):
            def block(index):
                i = (index * 205) >> 11
                j = (index - 10 * i) >> 1
                return a + i, j, index & 1

            def number(x, j, l):
                return (((((j - y_in_four) & 1) ^ y_role) * 2 + (l ^ z_role)) * 4) + jnp.minimum(x, 3)

            first = block(list_ref[a, k])
            second = block(list_ref[a, 56 + k])
            mine = (jnp.minimum(first[1], second[1]) == y_in_four) & (k < count)
            one_number, two_number = number(*first), number(*second)
            one_count, two_count = count_ref[one_number], count_ref[two_number]
            swap = (first[2] > second[2]) | ((first[2] == second[2]) & (one_count > two_count))
            sign = jnp.where(swap, -1, 1)
            left = jnp.where(swap, two_number, one_number)
            right = jnp.where(swap, one_number, two_number)
            steps = (jnp.where(swap, two_count, one_count) + (GROUP - 1)) // GROUP
            own_left = ((left >> 3) << 2) + (left & 3)
            word = own_left + right * 16 + (jnp.where(left == right, 1, 2) << 18)
            for place in range(3):
                word = word + ((sign * (first[place] - second[place]) + 1) << (12 + 2 * place))
            for step in range(128 // GROUP):
                out_ref[total + step] = word + step * 256
            return total + jnp.where(mine, steps, 0)

        def four(k, total, one=one):
            for part in range(4):
                total = one(4 * k + part, total)
            return total

        total = lax.fori_loop(0, (count + 3) // 4, four, total)
    for job in range(JOBS):
        out_ref[total + job] = 0
    total_ref[0] = (total + JOBS - 1) // JOBS
    total_ref[1] = z_role


def inverse_of(value):
    guess = pl.reciprocal(value, approx=True)
    return guess * (2.0 - value * guess)


def sweep_tiles(mode, list_ref, total_ref, rows_ref, columns_refs, row_sum_ref, column_sum_ref):
    forces, pulled = "F" in mode, "J" in mode
    made = 3 * forces + 4 * pulled

    def one_job(word):
        left, right, step = word & 15, (word >> 4) & 15, (word >> 8) & 15
        offset = [(((word >> (12 + 2 * c)) & 3) - 1).astype(jnp.float32) for c in range(3)]
        weight = (word >> 18).astype(jnp.float32) * 0.5

        def row(c, scale=None, shift=None):
            value = rows_ref[c, pl.ds(right, 1), :]
            if scale is not None:
                value = value * scale
            if shift is not None:
                value = value - shift
            return jnp.broadcast_to(value, (8, 128))

        right_pos = [row(c, shift=offset[c]) for c in range(3)]
        right_charge = row(3, scale=8.0 * weight)
        right_half = row(4)
        right_depth = row(5, scale=24.0 * weight)
        right_cot = [row(6 + c) for c in range(3)] if pulled else None

        sums = None
        for tile in range(TILES):
            eight = pl.ds(pl.multiple_of(left * 128 + step * GROUP + 8 * tile, 8), 8)

            def column(c):
                return columns_refs[c // 3][c % 3, eight, :]

            d = [column(c) - right_pos[c] for c in range(3)]
            charge = column(3)
            half = column(4) + right_half
            depth = column(5) * right_depth
            s = d[0] * d[0] + d[1] * d[1] + d[2] * d[2]
            sigma2 = half * half
            r = inverse_of(s + sigma2)
            t = sigma2 * r
            p = t * t * t
            soft = s + SOFT
            ir = lax.rsqrt(soft)
            g = jnp.exp2((soft * ir) * (-KAPPA * LOG2E)) * ir
            fade = jnp.maximum(1.0 - s, 0.0)
            fade2 = fade * fade
            fr = fade * r
            ir2 = ir * ir
            fade_kappa = fade * (ir + 0.5 * ir2)
            fade2h = fade2 * (g * (3.0 + fade_kappa))
            dp = depth * p
            charges = charge * right_charge
            A = (fade2 * dp) * ((p - 1.0) + fr * (2.0 * p - 1.0)) + charges * fade2h
            values = []
            if forces:
                values += [A * d[c] for c in range(3)]
            if pulled:
                w = [column(6 + c) - right_cot[c] for c in range(3)]
                dw = d[0] * w[0] + d[1] * w[1] + d[2] * w[2]
                lj = (2.0 * p - 2.0) + fr * ((12.0 * p - 6.0) + fr * (14.0 * p - 4.0))
                m2 = ir2 * (1.0 + 1.5 * ir + 0.75 * ir2)
                coulomb = 6.0 * (1.0 + fade_kappa) + fade2 * m2
                B = (-2.0 * fade) * (dp * lj + (charges * g) * coulomb) * dw
                values += [A * w[c] + B * d[c] for c in range(3)]
                common = fade2h * dw
                values += [common * right_charge]
                last = common * charge
            for place, value in enumerate(values):
                row_sum_ref[place, eight, :] = row_sum_ref[place, eight, :] + value
            if pulled:
                values[-1] = -last
            sums = values if sums is None else [a + b for a, b in zip(sums, values)]
        if pulled:
            sums[-1] = sums[-1] * (8.0 * weight)
        for place in range(made):
            column_sum_ref[place, right] = column_sum_ref[place, right] + sums[place]

    def one_step(k, carry):
        for job in range(JOBS):
            one_job(list_ref[k * JOBS + job])
        return carry

    lax.fori_loop(0, total_ref[0], one_step, jnp.int32(0))


def sweep_kernel(mode, first, kick, list_ref, total_ref, *refs):
    forces, pulled = "F" in mode, "J" in mode
    made = 3 * forces + 4 * pulled
    names = ["ext"] + (["params"] if not first or mode == "J" else []) + (["places"] if mode == "J" else [])
    if mode != "J":
        names += ["x", "v"] if not first else []
        names += [] if first else ["C", "rC", "D", "rD"]
    else:
        names += ["x", "ax", "av", "C", "rC", "D", "rD", "charge"] + (["v"] if first else [])
    outs = ["A", "B"] + (["places"] if mode != "J" else []) + (["params"] if mode == "F" and first else [])
    if mode == "F" and not first:
        outs += ["x_out", "v_out"]
    if mode == "FJ":
        outs += ["x_out", "v_out", "charge_out"]
    if mode == "J":
        outs += ["ax_out", "av_out", "charge_out"] + (["v_out"] if first else [])
    scratch = ["rows", "cotangents", "row_sum", "column_sum"]
    r = dict(zip(names + outs + scratch, refs))
    ext = r["ext"]
    inverse = ext[9]

    def received(c):
        return jnp.concatenate([r["C"][c] + r["rC"][c], r["D"][c] + r["rD"][c]], axis=0)

    position, cotangent = [], []
    for c in range(3):
        if mode != "J":
            if first:
                position.append(ext[c])
            else:
                velocity = r["v"][c] + kick * inverse * received(c)
                position.append(r["x"][c] + TIME_STEP * velocity)
                r["x_out"][c] = position[c]
                r["v_out"][c] = velocity
            if pulled:
                cotangent.append(HALF * inverse * ext[13 + c])
        else:
            if first:
                r["v_out"][c] = r["v"][c] + HALF * inverse * received(c)
            ax = r["ax"][c] + received(c + 3 if first else c)
            av = r["av"][c] + TIME_STEP * ax
            r["ax_out"][c] = ax
            r["av_out"][c] = av
            position.append(r["x"][c])
            cotangent.append(kick * inverse * av)
    _spread_and_sweep(mode, first, ext, position, cotangent, list_ref, total_ref, r, made, pulled)


def _spread_and_sweep(mode, first, ext, position, cotangent, list_ref, total_ref, r, made, pulled):
    rows = r["rows"]
    own_first = total_ref[1] == 0
    quantities = position + [ext[6], 0.5 * ext[7], ext[8]] + cotangent
    for place, value in enumerate(quantities):
        rows[place] = value
        fresh = (mode != "J", mode == "F" and first, True)[place // 3]
        if not fresh:
            continue
        target = (r["places"], r.get("params"), r["cotangents"])[place // 3]
        near = jnp.concatenate([value[0:4], value[8:12]], axis=0)
        far = jnp.concatenate([value[4:8], value[12:16]], axis=0)
        turned = jnp.where(own_first, near, far).T
        for e in range(OWN):
            target[place % 3, e * 128 : (e + 1) * 128, :] = jnp.broadcast_to(turned[:, e : e + 1], (128, 128))
    r["row_sum"][...] = jnp.zeros(r["row_sum"].shape, jnp.float32)
    r["column_sum"][...] = jnp.zeros(r["column_sum"].shape, jnp.float32)
    sweep_tiles(mode, list_ref, total_ref, rows, (r["places"], r["params"], r["cotangents"]), r["row_sum"], r["column_sum"])
    lane = lax.broadcasted_iota(jnp.int32, (128, OWN), 1)
    for c in range(made):
        by_atom = jnp.zeros((128, OWN), jnp.float32)
        for e in range(OWN):
            total = jnp.sum(r["row_sum"][c, e * 128 : (e + 1) * 128, :], axis=1, keepdims=True)
            by_atom = jnp.where(lane == e, jnp.broadcast_to(total, (128, OWN)), by_atom)
        own = by_atom.T
        others = jnp.sum(r["column_sum"][c], axis=1)
        A = jnp.where(own_first, own, 0.0) - jnp.concatenate([others[0:4], others[8:12]], axis=0)
        B = jnp.where(own_first, 0.0, own) - jnp.concatenate([others[4:8], others[12:16]], axis=0)
        if pulled and c == made - 1:
            total = jnp.concatenate([A[0:4], B[0:4], A[4:8], B[4:8]], axis=0)
            if mode == "J":
                total = total + r["charge"][...]
            r["charge_out"][...] = total
        else:
            r["A"][c] = A
            r["B"][c] = B


def sweep(mode, first, kick, plist, total, arrays):
    forces, pulled = "F" in mode, "J" in mode
    sent = 3 * forces + 3 * pulled
    made = 3 * forces + 4 * pulled
    quantities = 6 + 3 * pulled
    f32 = jnp.float32
    exchange = jax.ShapeDtypeStruct((sent, 8, 128), f32)
    vector = jax.ShapeDtypeStruct((3, BLOCKS, 128), f32)
    scalar = jax.ShapeDtypeStruct((BLOCKS, 128), f32)
    wide = jax.ShapeDtypeStruct((3, OWN * 128, 128), f32)
    outs = [exchange, exchange] + ([wide] if mode != "J" else []) + ([wide] if mode == "F" and first else [])
    if mode == "F" and not first:
        outs += [vector, vector]
    if mode == "FJ":
        outs += [vector, vector, scalar]
    if mode == "J":
        outs += [vector, vector, scalar] + ([vector] if first else [])
    vmem = pl.BlockSpec(memory_space=pltpu.VMEM)
    smem = pl.BlockSpec(memory_space=pltpu.SMEM)
    return pl.pallas_call(
        functools.partial(sweep_kernel, mode, first, kick),
        out_shape=outs,
        in_specs=[smem, smem] + [vmem] * len(arrays),
        out_specs=[vmem] * len(outs),
        scratch_shapes=[
            pltpu.VMEM((quantities, BLOCKS, 128), f32),
            pltpu.VMEM((3, OWN * 128 if pulled else 8, 128), f32),
            pltpu.VMEM((made, OWN * 128, 128), f32),
            pltpu.VMEM((made, BLOCKS, 8, 128), f32),
        ],
        compiler_params=pltpu.CompilerParams(vmem_limit_bytes=32 * 1024 * 1024),
        name=f"sweep_{mode}",
    )(plist, total, *arrays)


def exchanged(A, B):
    rA, rB = send(A, swap_pairs(1, 0)), send(B, swap_pairs(1, 1))
    T0, T1 = A + rA, B + rB
    C = jnp.concatenate([T0[:, 0:4], T1[:, 0:4]], axis=1)
    D = jnp.concatenate([T0[:, 4:8], T1[:, 4:8]], axis=1)
    return C, send(C, swap_pairs(0, 0)), D, send(D, swap_pairs(0, 1))


def on_device(
    positions,
    velocities,
    charges,
    atom_types,
    atom_count,
    sigma_type,
    epsilon_type,
    masses,
    pair_list,
    pair_count,
    pos_cotangent,
    vel_cotangent,
):
    f32 = jnp.float32
    a = lax.axis_index("gx")
    y, z = column_of_device()
    y_even, z_even = y % 2 == 0, z % 2 == 0
    counts = atom_count[0, :, 0]
    alive = (lax.broadcasted_iota(jnp.int32, (4, 128), 1) < counts[:, None]).astype(f32)
    kinds = (atom_types[0, :, 0][:, None, :] == lax.broadcasted_iota(jnp.int32, (16, 1), 0)).astype(f32)
    sigma = jnp.sum(kinds * sigma_type[:, None], axis=1)
    epsilon = jnp.sum(kinds * epsilon_type[:, None], axis=1)
    listed = jnp.concatenate(
        [pair_list[0, 0, 0].reshape(112), jnp.broadcast_to(pair_count[0, 0, 0], (16,))]
    ).astype(f32)
    bundle = jnp.concatenate(
        [
            positions[0, :, 0],
            velocities[0, :, 0],
            jnp.stack(
                [charges[0, :, 0] * alive, sigma, jnp.sqrt(epsilon) * alive, 1.0 / masses[0, :, 0]], axis=1
            ),
            pos_cotangent[0, :, 0],
            vel_cotangent[0, :, 0],
            jnp.broadcast_to(counts.astype(f32)[:, None, None], (4, 1, 128)),
            jnp.broadcast_to(listed[None, None, :], (4, 1, 128)),
        ],
        axis=1,
    )
    turned = lax.dynamic_slice_in_dim(jnp.concatenate([bundle, bundle]), a, 4)
    got = [send(turned[t], spread_pairs(t)) for t in range(4)]
    stacked = jnp.stack(got[::-1])
    y_in_four = y % 4
    own = lax.dynamic_slice_in_dim(jnp.concatenate([stacked, stacked]), 3 - y_in_four, 4)
    own = jnp.swapaxes(own, 0, 1)
    lists = own[17].astype(jnp.int32)
    own = own[:17]
    upper = send(own, down_pairs(1))
    wide = jnp.where(
        z_even, jnp.concatenate([upper, own], axis=1), jnp.concatenate([own, upper], axis=1)
    )
    upper = send(wide, down_pairs(0))
    ext = jnp.where(
        y_even, jnp.concatenate([upper, wide], axis=1), jnp.concatenate([wide, upper], axis=1)
    )
    y_role, z_role = jnp.where(y_even, 1, 0), jnp.where(z_even, 1, 0)
    smem = pl.BlockSpec(memory_space=pltpu.SMEM)
    plist, total = pl.pallas_call(
        list_kernel,
        out_shape=[jax.ShapeDtypeStruct((LIST,), jnp.int32), jax.ShapeDtypeStruct((2,), jnp.int32)],
        in_specs=[smem] * 3,
        out_specs=[smem] * 2,
        name="keep_pairs",
    )(
        lists,
        ext[16, :, 0].astype(jnp.int32),
        jnp.stack([y_in_four, y_role, z_role]).astype(jnp.int32),
    )
    A, B, places, params = sweep("F", True, 0.0, plist, total, [ext])
    history = [(ext[0:3], places)]
    x, v = ext[0:3], ext[3:6]
    for step in range(STEPS):
        parts = exchanged(A, B)
        kick = HALF if step == 0 else TIME_STEP
        mode = "F" if step < STEPS - 1 else "FJ"
        A, B, places, x, v, *rest = sweep(mode, False, kick, plist, total, [ext, params, x, v, *parts])
        history.append((x, places))
    charge = rest[0]
    ax, av = ext[10:13], ext[13:16]
    for step in range(STEPS - 1, -1, -1):
        parts = exchanged(A, B)
        first = step == STEPS - 1
        factor = TIME_STEP if step > 0 else HALF
        A, B, ax, av, charge, *rest = sweep(
            "J",
            first,
            factor,
            plist,
            total,
            [ext, params, history[step][1], history[step][0], ax, av, *parts, charge] + ([v] if first else []),
        )
        if first:
            v = rest[0]
    sides = charge.reshape(2, 2, 4, 128)
    A = jnp.concatenate([A, sides[:, 0].reshape(1, 8, 128)])
    B = jnp.concatenate([B, sides[:, 1].reshape(1, 8, 128)])
    C, rC, D, rD = exchanged(A, B)
    sums = jnp.concatenate([C + rC, D + rD], axis=1)
    whole = jnp.concatenate([x, v, ax + sums[:3], av, sums[3:4]])
    mine = lax.dynamic_slice_in_dim(whole, (y_role * 2 + z_role) * 4, 4, axis=1)
    mine = jnp.swapaxes(mine, 0, 1)
    turned = lax.dynamic_slice_in_dim(jnp.concatenate([mine, mine]), (y_in_four + 1) % 4, 4)
    got = [send(turned[3 - t], [(q, p) for p, q in spread_pairs(t)]) for t in range(4)]
    stacked = jnp.stack(got)
    out = lax.dynamic_slice_in_dim(jnp.concatenate([stacked, stacked]), (4 - a) % 4, 4)
    out = out[None, :, None]
    return (
        out[:, :, :, 0:3],
        out[:, :, :, 3:6],
        out[:, :, :, 6:9],
        out[:, :, :, 9:12],
        out[:, :, :, 12] * alive[None, :, None],
    )


def solution(mesh):
    vector = P("gx", "gy", "gz", None, None)
    scalar = P("gx", "gy", "gz", None)
    block = P("gx", "gy", "gz")
    in_specs = (
        vector, vector, scalar, scalar, block, P(), P(), scalar, vector, block, vector, vector,
    )
    out_specs = (vector, vector, vector, vector, scalar)
    return jax.shard_map(on_device, mesh=mesh, in_specs=in_specs, out_specs=out_specs, check_vma=False)
```
